32 devices in a mesh: tab: 8 (over z, y), col: 4 (over x, core).
Axes of the slice: x: 2, y: 2, z: 4, core: 2. Of those that a mesh axis runs over, the one named last changes fastest.
Arguments:
- bag_items: bfloat16 [128, 4, 48, 1024], P('tab', None, 'col'), may hold values from -3 to 3
- lengths: int32 [128, 1024], P('tab'), may hold values from 1 to 4
- field_slot: int32 [64], replicated, may hold values from 0 to 127, as said below
- filter_one: bfloat16 [32, 4096], replicated, may hold values from -0.09375 to 0.09375
- filter_two: bfloat16 [32, 2048], replicated, may hold values from -0.125 to 0.125
- cotangent: bfloat16 [64, 1024], P(None, ('tab', 'col')), may hold values from -12 to 12
Outputs:
- pooled: float32 [64, 1024], P(None, ('tab', 'col'))
- filter_grad_one: float32 [32, 4096], P(None, ('tab', 'col'))
- filter_grad_two: float32 [32, 2048], P(None, ('tab', 'col'))
- pooled_grad: bfloat16 [128, 48, 1024], P('tab', 'col')
The draws below stay inside these ranges and needn't reach their ends.
Inputs may be any that keep to these rules, and one draw needn't show every extreme that they name: Distinct values; the table of field f is held by index field_slot[f] // 16 of tab; owners hold 0 to 16 fields and one owner holds 16.
All inputs are finite; a program needn't handle non-finite values.
Results may differ from the reference program's by a relative error of at most 0.017.
Values may be sent and summed in bfloat16 or wider, within the bound.
No kernel may reach another device: no remote copies, remote signals or barrier semaphores. Data moves between devices by JAX's collectives and lax.ppermute only.
A program may use at most 64 MiB of HBM per device.

```python
import jax
import jax.numpy as jnp
from jax import lax

F = 64
D = 48
MAPS = 32
L_MAX = 4
SAMP_DEV = 128
SLOTS = 16
SAMPLES = 1024
N_TAB = 8


def draw_field_slot(key, part):
    slot_total = N_TAB * SLOTS
    owner_key, order_key, field_key = jax.random.split(jax.random.fold_in(key, 11), 3)
    full_owner = jax.random.randint(owner_key, (), 0, N_TAB)
    ranking = jax.random.permutation(order_key, slot_total).astype(jnp.int32)
    slot_index = jnp.arange(slot_total, dtype=jnp.int32)
    scores = jnp.where(slot_index // SLOTS == full_owner, slot_index - slot_total, ranking)
    chosen = jnp.argsort(scores, stable=True)[:F]
    shuffled = jax.random.permutation(field_key, F)
    return chosen[shuffled].astype(jnp.int32)


def plant(result, rng, smallest, largest):
    place = [jax.random.randint(jax.random.fold_in(rng, axis), (), 0, length) for axis, length in enumerate(result.shape)]
    widest = result.shape.index(max(result.shape))
    neighbour = place[:widest] + [(place[widest] + 1) % result.shape[widest]] + place[widest + 1:]
    return result.at[tuple(place)].set(smallest).at[tuple(neighbour)].set(largest)


def levels(key, extent, shards, low, top_value):
    def one(dim, shards_of):
        draws = jax.random.uniform(jax.random.fold_in(jax.random.fold_in(key, 6), dim), (shards_of,), jnp.float32, low / len(shards), top_value / len(shards))
        return jnp.repeat(jnp.exp(draws), extent[dim] // shards_of).reshape((-1,) + (1,) * (len(extent) - dim - 1))

    factor_of = one(*shards[0])
    for cut in shards[1:]:
        factor_of = factor_of * one(*cut)
    return factor_of


def bell_draw(own_key, shape, spread, bound, shards=(), kind=jnp.bfloat16):
    values = jax.random.normal(own_key, shape, jnp.float32) * spread
    if len(shards) > 0:
        values = levels(own_key, shape, shards, -0.22, 0.18) * values
    return jnp.clip(values, min=-bound, max=bound).astype(kind)


def setup_inputs(seed: int = 0) -> dict:
    arg_keys = jax.random.split(jax.random.key(seed), 7)
    return {
        "bag_items": bell_draw(arg_keys[0], (N_TAB * SLOTS, L_MAX, D, SAMPLES), 0.5, 3.0, ((0, 8), (2, 4))),
        "lengths": plant(jax.random.randint(arg_keys[1], (N_TAB * SLOTS, SAMPLES), 1, L_MAX + 1), jax.random.fold_in(arg_keys[1], 1), 1, L_MAX).astype(jnp.int32),
        "field_slot": draw_field_slot(jax.random.fold_in(arg_keys[6], 71), 0),
        "filter_one": bell_draw(arg_keys[3], (MAPS, F * F), (F * F) ** -0.5, 0.09375),
        "filter_two": bell_draw(arg_keys[4], (MAPS, MAPS * F), (MAPS * F) ** -0.5, 0.125),
        "cotangent": bell_draw(arg_keys[5], (2 * MAPS, SAMPLES), 2.0, 12.0, ((1, 32),)),
    }


def cross_block(first_cols, upstream, filter_one, filter_two):
    fields, columns = first_cols.shape
    map_count = filter_one.shape[0]
    first_pairs = (first_cols[:, None, :] * first_cols[None, :, :]).reshape(fields * fields, columns)
    first_maps = jnp.dot(filter_one, first_pairs, preferred_element_type=jnp.float32)
    hidden_cols = lax.optimization_barrier(first_maps.astype(jnp.bfloat16))
    second_pairs = (hidden_cols[:, None, :] * first_cols[None, :, :]).reshape(map_count * fields, columns)
    second_maps = jnp.dot(filter_two, second_pairs, preferred_element_type=jnp.float32)
    upper_grad = upstream[map_count:]
    grad_two = lax.dot_general(upper_grad, second_pairs, (((1,), (1,)), ((), ())), preferred_element_type=jnp.float32)
    pair_grad_two = lax.dot_general(filter_two, upper_grad, (((0,), (0,)), ((), ())), preferred_element_type=jnp.float32)
    pair_grad_two = lax.optimization_barrier(pair_grad_two.astype(jnp.bfloat16))
    pair_grad_two = pair_grad_two.reshape(map_count, fields, columns).astype(jnp.float32)
    first_float = first_cols.astype(jnp.float32)
    hidden_grad = jnp.sum(pair_grad_two * first_float[None], axis=1)
    field_grad = jnp.sum(pair_grad_two * hidden_cols.astype(jnp.float32)[:, None], axis=0)
    lower_grad = (upstream[:map_count].astype(jnp.float32) + hidden_grad).astype(jnp.bfloat16)
    grad_one = lax.dot_general(lower_grad, first_pairs, (((1,), (1,)), ((), ())), preferred_element_type=jnp.float32)
    pair_grad_one = lax.dot_general(filter_one, lower_grad, (((0,), (0,)), ((), ())), preferred_element_type=jnp.float32)
    pair_grad_one = lax.optimization_barrier(pair_grad_one.astype(jnp.bfloat16))
    pair_grad_one = pair_grad_one.reshape(fields, fields, columns).astype(jnp.float32)
    field_grad = field_grad + jnp.sum(pair_grad_one * first_float[None], axis=1) + jnp.sum(pair_grad_one * first_float[:, None], axis=0)
    return first_maps, second_maps, field_grad.astype(jnp.bfloat16), grad_one, grad_two


def reference(bag_items, lengths, field_slot, filter_one, filter_two, cotangent):
    item_index = jnp.arange(L_MAX)[None, :, None, None]
    kept_items = jnp.where(item_index < lengths[:, None, None, :], bag_items, jnp.zeros_like(bag_items))
    pooled_table = jnp.sum(kept_items.astype(jnp.float32), axis=1).astype(jnp.bfloat16)
    field_embed = pooled_table[field_slot]
    block_count = SAMPLES // SAMP_DEV
    embed_blocks = field_embed.reshape(F, D, block_count, SAMP_DEV).transpose(2, 0, 1, 3).reshape(block_count, F, D * SAMP_DEV)
    grad_blocks = cotangent.reshape(2 * MAPS, block_count, SAMP_DEV).transpose(1, 0, 2)

    def advance(totals, inputs):
        embed_cols, grad_cols = inputs
        upstream = jnp.broadcast_to(grad_cols[:, None, :], (2 * MAPS, D, SAMP_DEV)).astype(jnp.float32) * D ** -0.5
        upstream = upstream.astype(jnp.bfloat16).reshape(2 * MAPS, D * SAMP_DEV)
        first_maps, second_maps, field_grad, grad_one, grad_two = cross_block(embed_cols, upstream, filter_one, filter_two)
        both_maps = jnp.concatenate([first_maps, second_maps], axis=0).reshape(2 * MAPS, D, SAMP_DEV)
        pooled_cols = jnp.sum(both_maps, axis=1) * D ** -0.5
        return (totals[0] + grad_one, totals[1] + grad_two), (pooled_cols, field_grad)

    zero_sums = (jnp.zeros((MAPS, F * F), jnp.float32), jnp.zeros((MAPS, MAPS * F), jnp.float32))
    (grad_one, grad_two), (pooled_blocks, field_blocks) = lax.scan(advance, zero_sums, (embed_blocks, grad_blocks))
    pooled = pooled_blocks.transpose(1, 0, 2).reshape(2 * MAPS, SAMPLES)
    field_grad = field_blocks.reshape(block_count, F, D, SAMP_DEV).transpose(1, 2, 0, 3).reshape(F, D, SAMPLES)
    pooled_grad = jnp.zeros((N_TAB * SLOTS, D, SAMPLES), jnp.bfloat16).at[field_slot].set(field_grad)
    grad_scale = SAMPLES ** -0.5
    return pooled, grad_one * grad_scale, grad_two * grad_scale, pooled_grad
```

```python
import functools

import jax
import jax.numpy as jnp
from jax import lax
from jax.experimental import pallas as pl
from jax.experimental.pallas import tpu as pltpu
from jax.sharding import PartitionSpec as P

BF16 = jnp.bfloat16
F32 = jnp.float32
VMEM_BYTES = 48 * 1024 * 1024
MATMUL_ROWS = 512


def params():
    return pltpu.CompilerParams(vmem_limit_bytes=VMEM_BYTES)


def cost(flops, moved):
    return pl.CostEstimate(flops=flops, bytes_accessed=moved, transcendentals=0)


def whole():
    return pl.BlockSpec(memory_space=pltpu.VMEM)


def dot(left, right):
    return jnp.dot(left, right, preferred_element_type=F32)


def dot_lanes(left, right):
    return lax.dot_general(left, right, (((1,), (1,)), ((), ())), preferred_element_type=F32)


def pool_kernel(bag_ref, lengths_ref, out_ref, rows_ref):
    slots, items, width, _ = bag_ref.shape
    chunks, _, lanes = out_ref.shape
    for chunk in range(chunks):
        here = pl.ds(chunk * lanes, lanes)
        for slot in range(slots):
            count = lengths_ref[slot : slot + 1, here]
            total = jnp.zeros((width, lanes), F32)
            for item in range(items):
                value = bag_ref[slot, item, :, here].astype(F32)
                total = total + jnp.where(count > item, value, 0.0)
            rows_ref[pl.ds(slot, width, stride=slots), :] = total
        out_ref[chunk] = rows_ref[...].astype(BF16)


def pool(bag_items, lengths, tab_count):
    slots, items, width, samples = bag_items.shape
    lanes = samples // tab_count
    steps = min(4, tab_count)
    per_step = tab_count // steps
    return pl.pallas_call(
        pool_kernel,
        grid=(steps,),
        in_specs=[
            pl.BlockSpec((slots, items, width, per_step * lanes), lambda i: (0, 0, 0, i)),
            pl.BlockSpec((slots, per_step * lanes), lambda i: (0, i)),
        ],
        out_specs=pl.BlockSpec((per_step, width * slots, lanes), lambda i: (i, 0, 0)),
        out_shape=jax.ShapeDtypeStruct((tab_count, width * slots, lanes), BF16),
        scratch_shapes=[pltpu.VMEM((width * slots, lanes), F32)],
        compiler_params=params(),
        name="pool_bags",
    )(bag_items, lengths)


def field_rows(received_ref, onehot, column, slots):
    parts = [
        received_ref[t, pl.ds(pl.multiple_of(column * slots, slots), slots), :]
        for t in range(received_ref.shape[0])
    ]
    rows = parts[0] if len(parts) == 1 else jnp.concatenate(parts, axis=0)
    return dot(onehot, rows)


def filter_kernel(
    packed, scales,
    col_ref, received_ref, slot_ref, cot_ref, sym_ref, second_ref,
    *refs,
):
    out_count = packed[0] if packed else 2
    outs = refs[:out_count]
    embed_ref, hidden_ref, lower_ref = refs[out_count : out_count + 3]
    up_ref, z_ref, x_ref, h_ref, pooled_ref, grad_ref, pack_ref = refs[out_count + 3 :]
    fields = slot_ref.shape[0]
    maps, positions = hidden_ref.shape
    lanes = cot_ref.shape[1]
    width = positions // lanes
    slots = received_ref.shape[1] // width
    pair = 2 * lanes
    all_slots = received_ref.shape[0] * slots
    scale = scales[0]
    onehot = (lax.broadcasted_iota(jnp.int32, (fields, all_slots), 1) == slot_ref[...]).astype(BF16)
    up = (cot_ref[...].astype(F32) * scale).astype(BF16).astype(F32)
    up_ref[:, :lanes] = up
    up_ref[:, lanes:] = up
    pooled_ref[...] = jnp.zeros_like(pooled_ref)
    grad_ref[...] = jnp.zeros_like(grad_ref)

    def step(index, carry):
        here = pl.ds(pl.multiple_of(index * pair, pair), pair)
        x_float = jnp.concatenate(
            [field_rows(received_ref, onehot, 2 * index + k, slots) for k in range(2)], axis=1
        )
        x_ref[...] = x_float
        x = x_float.astype(BF16)
        embed_ref[:, here] = x
        hidden_grad = jnp.zeros((maps, pair), F32)
        rows = min(MATMUL_ROWS, maps * maps)
        for start in range(0, maps * maps, rows):
            z = dot(second_ref[start : start + rows, :], x)
            z_ref[start : start + rows, :] = z
            for k in range(rows // maps):
                o = start // maps + k
                hidden_grad = hidden_grad + up_ref[maps + o : maps + o + 1, :] * z[k * maps : (k + 1) * maps]
        lower = (up_ref[:maps, :] + hidden_grad).astype(BF16)
        lower_ref[:, here] = lower
        lower = lower.astype(F32)
        rows = min(MATMUL_ROWS, maps * fields)
        for start in range(0, maps * fields, rows):
            y = dot(sym_ref[start : start + rows, :], x).reshape(rows // fields, fields, pair)
            o = start // fields
            h_ref[o : o + rows // fields, :] = 0.5 * jnp.sum(y * x_float[None], axis=1)
        first_maps = h_ref[...]
        pooled_ref[:maps, :] += first_maps
        hidden = first_maps.astype(BF16)
        hidden_ref[:, here] = hidden
        hidden = hidden.astype(F32)
        h_ref[...] = hidden
        for o in range(maps):
            total = jnp.sum(z_ref[o * maps : (o + 1) * maps, :] * hidden, axis=0, keepdims=True)
            pooled_ref[maps + o : maps + o + 1, :] += total
        group = MATMUL_ROWS // maps
        for first in range(0, fields, group):
            pairs = jnp.concatenate(
                [(x_ref[first + k : first + k + 1, :] * lower).astype(BF16) for k in range(group)], axis=0
            )
            grad_ref[first * maps : (first + group) * maps, :] += dot_lanes(pairs, x)
        upper = up_ref[maps:, :]
        base = fields * maps
        for first in range(0, maps, group):
            pairs = jnp.concatenate(
                [(h_ref[first + k : first + k + 1, :] * upper).astype(BF16) for k in range(group)], axis=0
            )
            grad_ref[base + first * maps : base + (first + group) * maps, :] += dot_lanes(pairs, x)
        return carry

    lax.fori_loop(0, width // 2, step, 0)
    pooled = (pooled_ref[:, :lanes] + pooled_ref[:, lanes:]) * scale
    if not packed:
        outs[0][...] = grad_ref[...] * scales[1]
        outs[1][...] = pooled
        return
    cols, tabs = packed
    share = lanes // cols
    tall = 2 * maps * share // lanes
    for c in range(cols):
        pack_ref[c] = jnp.concatenate(
            [
                pooled[g * tall : (g + 1) * tall, c * share : (c + 1) * share]
                for g in range(lanes // share)
            ],
            axis=1,
        )
    own = col_ref[0]
    block = maps + maps // 2
    for r in range(cols):
        c = jnp.bitwise_xor(own, r)
        for t in range(tabs):
            k = t * cols + c
            at = pl.multiple_of(k * 2 * maps, 2 * maps)
            first = grad_ref[pl.ds(at, 2 * maps), :]
            first = jnp.concatenate([first[:maps], first[maps:]], axis=1)
            at = pl.multiple_of(base_rows(fields, maps) + k * maps, maps)
            second = grad_ref[pl.ds(at, maps), :]
            second = jnp.concatenate([second[: maps // 2], second[maps // 2 :]], axis=1)
            outs[r][t * block : (t + 1) * block, :] = (
                jnp.concatenate([first, second], axis=0) * scales[1]
            ).astype(BF16)
        outs[r][tabs * block :, :] = pack_ref[c].astype(BF16)


def base_rows(fields, maps):
    return fields * maps


def filter_part(packed, scales, col, received, slot, cot, sym, second, width):
    fields = slot.shape[0]
    maps = cot.shape[0] // 2
    lanes = cot.shape[1]
    positions = width * lanes
    pair = 2 * lanes
    kept = [
        jax.ShapeDtypeStruct((fields, positions), BF16),
        jax.ShapeDtypeStruct((maps, positions), BF16),
        jax.ShapeDtypeStruct((maps, positions), BF16),
    ]
    grads = (fields + maps) * maps
    if packed:
        cols, tabs = packed
        tall = 2 * maps // cols
        piece = (tabs * (maps + maps // 2) + tall, lanes)
        outs = [jax.ShapeDtypeStruct(piece, BF16)] * cols
        pack = pltpu.VMEM((cols, tall, lanes), F32)
    else:
        outs = [
            jax.ShapeDtypeStruct((grads, fields), F32),
            jax.ShapeDtypeStruct((2 * maps, lanes), F32),
        ]
        pack = pltpu.VMEM((1, 8, lanes), F32)
    return pl.pallas_call(
        functools.partial(filter_kernel, packed, scales),
        in_specs=[pl.BlockSpec(memory_space=pltpu.SMEM)] + [whole()] * 5,
        out_specs=[whole()] * (len(outs) + 3),
        out_shape=outs + kept,
        scratch_shapes=[
            pltpu.VMEM((2 * maps, pair), F32),
            pltpu.VMEM((maps * maps, pair), F32),
            pltpu.VMEM((fields, pair), F32),
            pltpu.VMEM((maps, pair), F32),
            pltpu.VMEM((2 * maps, pair), F32),
            pltpu.VMEM((grads, fields), F32),
            pack,
        ],
        compiler_params=params(),
        cost_estimate=cost(8 * maps * fields * fields * positions, 4 * received.size),
        name="filter_part",
    )(col, received, slot, cot, sym, second)


def embed_kernel(
    scale, slots, slot_ref, cot_ref, sym_ref, turned_ref, embed_ref, hidden_ref, lower_ref,
    out_ref, up_ref, low_ref, hid_ref, pair_ref,
):
    fields = slot_ref.shape[1]
    maps, positions = hidden_ref.shape
    lanes = cot_ref.shape[1]
    width = positions // lanes
    tabs = out_ref.shape[0]
    all_slots = tabs * slots
    pair = 2 * lanes
    spread = (lax.broadcasted_iota(jnp.int32, (all_slots, fields), 0) == slot_ref[...]).astype(BF16)
    up = (cot_ref[maps:, :].astype(F32) * scale).astype(BF16).astype(F32)
    up_ref[:, :lanes] = up
    up_ref[:, lanes:] = up

    def step(index, carry):
        here = pl.ds(pl.multiple_of(index * pair, pair), pair)
        x = embed_ref[:, here]
        low_ref[...] = lower_ref[:, here].astype(F32)
        hid_ref[...] = hidden_ref[:, here].astype(F32)
        upper = up_ref[...]
        for h in range(maps):
            pair_ref[h * maps : (h + 1) * maps, :] = (hid_ref[h : h + 1, :] * upper).astype(BF16)
        total = dot(turned_ref[...], pair_ref[...])
        rows = min(MATMUL_ROWS, maps * fields)
        for start in range(0, maps * fields, rows):
            y = dot(sym_ref[start : start + rows, :], x)
            for k in range(rows // fields):
                o = start // fields + k
                total = total + low_ref[o : o + 1, :] * y[k * fields : (k + 1) * fields]
        table = dot(spread, total.astype(BF16)).astype(BF16)
        for k in range(2):
            at = pl.ds(pl.multiple_of((2 * index + k) * slots, slots), slots)
            for t in range(tabs):
                out_ref[t, at, :] = table[t * slots : (t + 1) * slots, k * lanes : (k + 1) * lanes]
        return carry

    lax.fori_loop(0, width // 2, step, 0)


def embed_part(scale, slots, slot_row, cot, sym, turned, embed, hidden, lower, tabs, rows, width):
    fields = slot_row.shape[1]
    maps = hidden.shape[0]
    lanes = cot.shape[1]
    pair = 2 * lanes
    return pl.pallas_call(
        functools.partial(embed_kernel, scale, slots),
        in_specs=[whole()] * 7,
        out_specs=whole(),
        out_shape=jax.ShapeDtypeStruct((tabs, rows, lanes), BF16),
        scratch_shapes=[
            pltpu.VMEM((maps, pair), F32),
            pltpu.VMEM((maps, pair), F32),
            pltpu.VMEM((maps, pair), F32),
            pltpu.VMEM((maps * maps, pair), BF16),
        ],
        compiler_params=params(),
        cost_estimate=cost(4 * maps * fields * fields * width * lanes, 4 * tabs * rows * lanes),
        name="embed_part",
    )(slot_row, cot, sym, turned, embed, hidden, lower)


def owner_kernel(table_ref, out_ref, rows_ref):
    slots, width, _ = out_ref.shape
    tabs, _, lanes = table_ref.shape
    for t in range(tabs):
        rows_ref[...] = table_ref[t, : width * slots, :].astype(F32)
        for slot in range(slots):
            value = rows_ref[pl.ds(slot, width, stride=slots), :]
            out_ref[slot, :, pl.ds(t * lanes, lanes)] = value.astype(BF16)


def owner_part(table, slots, width):
    tabs, _, lanes = table.shape
    return pl.pallas_call(
        owner_kernel,
        in_specs=[whole()],
        out_specs=whole(),
        out_shape=jax.ShapeDtypeStruct((slots, width, tabs * lanes), BF16),
        scratch_shapes=[pltpu.VMEM((width * slots, lanes), F32)],
        compiler_params=params(),
        name="owner_part",
    )(table)


def per_device(bag_items, lengths, field_slot, filter_one, filter_two, cotangent):
    slots, _, width, samples = bag_items.shape
    tabs = lax.axis_size("tab")
    cols = lax.axis_size("col")
    devices = tabs * cols
    lanes = samples // tabs
    maps = filter_one.shape[0]
    fields = field_slot.shape[0]
    scale = (width * cols) ** -0.5
    scales = (scale, samples**-0.5)
    sent = pool(bag_items, lengths, tabs)
    received = lax.all_to_all(sent, "tab", split_axis=0, concat_axis=0, tiled=True)
    cot = lax.all_gather(cotangent, "col", axis=1, tiled=True)
    square = filter_one.reshape(maps, fields, fields).astype(F32)
    sym = (square + square.transpose(0, 2, 1)).astype(BF16).reshape(maps * fields, fields)
    second = filter_two.reshape(maps * maps, fields)
    turned = filter_two.reshape(maps, maps, fields).transpose(2, 1, 0).reshape(fields, maps * maps)
    small = slots % 16 != 0
    if small:
        received = received.reshape(tabs, width, slots, lanes).transpose(1, 0, 2, 3)
        received = received.reshape(1, width * tabs * slots, lanes)
    packable = (
        fields * fields == devices * lanes
        and fields * 2 == lanes
        and maps == devices
        and cols & (cols - 1) == 0
        and not small
    )
    col = lax.axis_index("col").astype(jnp.int32).reshape(1)
    results = filter_part(
        (cols, tabs) if packable else None,
        scales, col, received, field_slot.reshape(fields, 1), cot, sym, second, width,
    )
    embed, hidden, lower = results[-3:]
    table_rows = received.shape[1]
    block = maps + maps // 2
    if packable:
        parts = [results[0]]
        for r in range(1, cols):
            parts.append(lax.ppermute(results[r], "col", [(c, c ^ r) for c in range(cols)]))
        table = embed_part(
            scale, slots, field_slot.reshape(1, fields), cot, sym, turned, embed, hidden, lower,
            tabs, table_rows + block, width,
        )
        total = functools.reduce(lambda a, b: a + b, [part.astype(F32) for part in parts])
        grads = total[: tabs * block].astype(BF16).reshape(tabs, block, lanes)
        table = lax.dynamic_update_slice(table, grads, (0, table_rows, 0))
        returned = lax.all_to_all(table, "tab", split_axis=0, concat_axis=0, tiled=True)
        pooled_grad = owner_part(returned, slots, width)
        grads = jnp.sum(returned[:, table_rows:, :].astype(F32), axis=0)
        grad_one = grads[:maps]
        grad_two = jnp.concatenate([grads[maps:, :fields], grads[maps:, fields:]], axis=0)
        share = lanes // cols
        packs = total[tabs * block :]
        pooled = jnp.concatenate(
            [packs[:, g * share : (g + 1) * share] for g in range(lanes // share)], axis=0
        )
        return (pooled, grad_one, grad_two, pooled_grad)
    table = embed_part(
        scale, table_rows // width, field_slot.reshape(1, fields), cot, sym, turned, embed, hidden, lower,
        received.shape[0], table_rows, width,
    )
    if small:
        table = table.reshape(width, tabs, slots, lanes).transpose(1, 0, 2, 3)
        table = table.reshape(tabs, width * slots, lanes)
    returned = lax.all_to_all(table, "tab", split_axis=0, concat_axis=0, tiled=True)
    pooled_grad = owner_part(returned, slots, width)
    pooled = lax.psum_scatter(results[1], "col", scatter_dimension=1, tiled=True)
    shaped = results[0].reshape(fields + maps, maps, fields).transpose(1, 0, 2)
    grad_one = shaped[:, :fields].reshape(maps, tabs, cols, -1)
    grad_two = shaped[:, fields:].reshape(maps, tabs, cols, -1)
    grad_one = lax.psum_scatter(grad_one, "col", scatter_dimension=2, tiled=True)
    grad_two = lax.psum_scatter(grad_two, "col", scatter_dimension=2, tiled=True)
    grad_one = lax.psum_scatter(grad_one, "tab", scatter_dimension=1, tiled=True)
    grad_two = lax.psum_scatter(grad_two, "tab", scatter_dimension=1, tiled=True)
    return (pooled, grad_one.reshape(maps, -1), grad_two.reshape(maps, -1), pooled_grad)


def solution(mesh):
    in_specs = (P("tab", None, "col", None), P("tab", None), P(), P(), P(), P(None, ("tab", "col")))
    out_specs = (
        P(None, ("tab", "col")),
        P(None, ("tab", "col")),
        P(None, ("tab", "col")),
        P("tab", "col", None),
    )
    return jax.shard_map(
        per_device, mesh=mesh, in_specs=in_specs, out_specs=out_specs, check_vma=False
    )
```

```python
import functools

import jax
import jax.numpy as jnp
from jax import lax
from jax.experimental import pallas as pl
from jax.experimental.pallas import tpu as pltpu
from jax.sharding import PartitionSpec as P

BF16 = jnp.bfloat16
F32 = jnp.float32
VMEM_BYTES = 48 * 1024 * 1024
MATMUL_ROWS = 512


def params():
    return pltpu.CompilerParams(vmem_limit_bytes=VMEM_BYTES)


def cost(flops, moved):
    return pl.CostEstimate(flops=flops, bytes_accessed=moved, transcendentals=0)


def whole():
    return pl.BlockSpec(memory_space=pltpu.VMEM)


def dot(left, right):
    return jnp.dot(left, right, preferred_element_type=F32)


def dot_lanes(left, right):
    return lax.dot_general(left, right, (((1,), (1,)), ((), ())), preferred_element_type=F32)


def pool_kernel(steps, bag_hbm, lengths_hbm, out_ref, bag_ref, lengths_ref, rows_ref, sems):
    slots, width, items, _ = bag_hbm.shape
    chunks, _, lanes = out_ref.shape
    per_step = chunks // steps
    counts = pltpu.make_async_copy(lengths_hbm, lengths_ref, sems.at[steps])
    counts.start()
    copies = []
    for k in range(steps):
        part = pl.ds(k * per_step * lanes, per_step * lanes)
        copy = pltpu.make_async_copy(
            bag_hbm.at[:, :, :, part], bag_ref.at[:, :, :, part], sems.at[k]
        )
        copy.start()
        copies.append(copy)
    counts.wait()
    for chunk in range(chunks):
        if chunk % per_step == 0:
            copies[chunk // per_step].wait()
        here = pl.ds(chunk * lanes, lanes)
        buffer = chunk % 2
        for slot in range(slots):
            at = slot * width * items
            rows_ref[buffer, at : at + width * items, :] = (
                bag_ref[slot, :, :, here].astype(F32).reshape(width * items, lanes)
            )
        count = lengths_ref[:, here]
        for d in range(width):
            total = jnp.zeros((slots, lanes), F32)
            for item in range(items):
                value = rows_ref[buffer, pl.ds(d * items + item, slots, stride=width * items), :]
                total = total + jnp.where(count > item, value, 0.0)
            out_ref[chunk, d * slots : (d + 1) * slots, :] = total.astype(BF16)


def pool(bag_items, lengths, tab_count):
    bag = bag_items.transpose(0, 2, 1, 3)
    slots, width, items, samples = bag.shape
    lanes = samples // tab_count
    steps = min(4, tab_count)
    return pl.pallas_call(
        functools.partial(pool_kernel, steps),
        in_specs=[pl.BlockSpec(memory_space=pltpu.HBM)] * 2,
        out_specs=whole(),
        out_shape=jax.ShapeDtypeStruct((tab_count, width * slots, lanes), BF16),
        scratch_shapes=[
            pltpu.VMEM(bag.shape, BF16),
            pltpu.VMEM(lengths.shape, jnp.int32),
            pltpu.VMEM((2, width * slots * items, lanes), F32),
            pltpu.SemaphoreType.DMA((steps + 1,)),
        ],
        compiler_params=pltpu.CompilerParams(vmem_limit_bytes=62 * 1024 * 1024),
        name="pool_bags",
    )(bag, lengths)


def embed_kernel(
    scale,
    received_ref, slot_ref, slot_row_ref, cot_ref, sym_ref, second_ref, inner_ref,
    table_ref, embed_ref, hidden_ref, lower_ref, one_ref,
    up_ref, x_ref, low_ref, maps_ref, sum_ref, buf_ref,
):
    fields = slot_ref.shape[0]
    maps, positions = hidden_ref.shape
    lanes = cot_ref.shape[1]
    width = positions // lanes
    tabs = received_ref.shape[0]
    slots = received_ref.shape[1] // width
    pair = 2 * lanes
    all_slots = tabs * slots
    onehot = (lax.broadcasted_iota(jnp.int32, (fields, all_slots), 1) == slot_ref[...]).astype(BF16)
    spread = (
        lax.broadcasted_iota(jnp.int32, (all_slots, fields), 0) == slot_row_ref[...]
    ).astype(BF16)
    up = (cot_ref[...].astype(F32) * scale).astype(BF16).astype(F32)
    up_ref[:, :lanes] = up
    up_ref[:, lanes:] = up
    for d in range(width):
        parts = [received_ref[t, d * slots : (d + 1) * slots, :] for t in range(tabs)]
        x = dot(onehot, parts[0] if len(parts) == 1 else jnp.concatenate(parts, axis=0))
        x_ref[:, d * lanes : (d + 1) * lanes] = x
        embed_ref[:, d * lanes : (d + 1) * lanes] = x.astype(BF16)
    sum_ref[...] = jnp.zeros_like(sum_ref)

    rows = 1024
    jobs = []
    for p in range(width // 2):
        jobs += [("z", p, start) for start in range(0, maps * maps, rows)]
        jobs += [("y", p, start) for start in range(0, maps * fields, rows)]

    def issue(number):
        kind, p, start = jobs[number]
        source = second_ref if kind == "z" else sym_ref
        x = embed_ref[:, p * pair : (p + 1) * pair]
        buf_ref[number % 2] = dot(source[start : start + rows, :], x)

    state = {}
    def consume(number):
        kind, p, start = jobs[number]
        here = pl.ds(p * pair, pair)
        b = p % 2
        y_ref = buf_ref.at[number % 2]
        if kind == "z":
            lower = up_ref[:maps, :] if start == 0 else state["lower"]
            for k in range(rows // maps):
                o = start // maps + k
                lower = lower + up_ref[maps + o : maps + o + 1, :] * y_ref[k * maps : (k + 1) * maps, :]
            state["lower"] = lower
            if start + rows == maps * maps:
                lower = lower.astype(BF16)
                lower_ref[:, here] = lower
                low_ref[b] = lower.astype(F32)
            return
        gradient = jnp.zeros((fields, pair), F32) if start == 0 else state["gradient"]
        x_float = x_ref[:, here]
        for k in range(rows // fields):
            o = start // fields + k
            mine = y_ref[k * fields : (k + 1) * fields, :]
            gradient = gradient + low_ref[b, o : o + 1, :] * mine
            maps_ref[b, o : o + 1, :] = 0.5 * jnp.sum(mine * x_float, axis=0, keepdims=True)
        state["gradient"] = gradient
        if start + rows < maps * fields:
            return
        first_maps = maps_ref[b]
        sum_ref[...] += first_maps
        hidden = first_maps.astype(BF16)
        hidden_ref[:, here] = hidden
        maps_ref[b] = hidden.astype(F32)
        sides = [gradient[:, :lanes], gradient[:, lanes:]]
        for h in range(maps):
            inner = inner_ref[h * fields : (h + 1) * fields, :]
            for k in range(2):
                sides[k] = sides[k] + maps_ref[b, h : h + 1, k * lanes : (k + 1) * lanes] * inner
        for k in range(2):
            table = dot(spread, sides[k].astype(BF16)).astype(BF16)
            at = (2 * p + k) * slots
            for t in range(tabs):
                table_ref[t, at : at + slots, :] = table[t * slots : (t + 1) * slots, :]

    ahead = 1
    for number in range(ahead):
        issue(number)
    for number in range(len(jobs)):
        if number + ahead < len(jobs):
            issue(number + ahead)
        consume(number)
    one_ref[...] = sum_ref[:, :lanes] + sum_ref[:, lanes:]


def embed_part(scale, received, slot, cot, sym, second, inner, width):
    fields = slot.shape[0]
    maps = cot.shape[0] // 2
    lanes = cot.shape[1]
    positions = width * lanes
    pair = 2 * lanes
    return pl.pallas_call(
        functools.partial(embed_kernel, scale),
        in_specs=[whole()] * 7,
        out_specs=[whole()] * 5,
        out_shape=[
            jax.ShapeDtypeStruct(received.shape, BF16),
            jax.ShapeDtypeStruct((fields, positions), BF16),
            jax.ShapeDtypeStruct((maps, positions), BF16),
            jax.ShapeDtypeStruct((maps, positions), BF16),
            jax.ShapeDtypeStruct((maps, lanes), F32),
        ],
        scratch_shapes=[
            pltpu.VMEM((2 * maps, pair), F32),
            pltpu.VMEM((fields, positions), F32),
            pltpu.VMEM((2, maps, pair), F32),
            pltpu.VMEM((2, maps, pair), F32),
            pltpu.VMEM((maps, pair), F32),
            pltpu.VMEM((2, 1024, pair), F32),
        ],
        compiler_params=params(),
        cost_estimate=cost(8 * maps * fields * fields * positions, 4 * received.size),
        name="embed_part",
    )(received, slot.reshape(fields, 1), slot.reshape(1, fields), cot, sym, second, inner)


def filter_kernel(
    packed, scales, place_ref, cot_ref, second_ref, embed_ref, hidden_ref, lower_ref, one_ref, *refs
):
    outs = refs[:2]
    x_ref, hid_ref, inner_ref, grad_ref, pair_ref, pack_ref = refs[2:]
    fields = embed_ref.shape[0]
    maps, positions = hidden_ref.shape
    lanes = cot_ref.shape[1]
    width = positions // lanes
    pair = 2 * lanes
    scale = scales[0]
    up = (cot_ref[maps:, :].astype(F32) * scale).astype(BF16)
    x_ref[...] = embed_ref[...].astype(F32)
    hid_ref[...] = hidden_ref[...].astype(F32)
    rows = 512
    steps = [
        (p, start) for p in range(width // 2) for start in range(0, fields * maps, rows)
    ]

    def products(number):
        p, start = steps[number]
        here = pl.ds(p * pair, pair)
        lower = lower_ref[:, here].astype(F32)
        for k in range(rows // maps):
            f = start // maps + k
            pair_ref[number % 2, k * maps : (k + 1) * maps, :] = (
                x_ref[f : f + 1, here] * lower
            ).astype(BF16)

    def sums(number):
        p, start = steps[number]
        part = dot_lanes(pair_ref[number % 2], embed_ref[:, p * pair : (p + 1) * pair])
        if p == 0:
            grad_ref[start : start + rows, :] = part
        else:
            grad_ref[start : start + rows, :] += part

    def inner(first, count):
        totals = [jnp.zeros((fields, lanes), F32)] * count
        for d in range(width):
            here = pl.ds(d * lanes, lanes)
            x = x_ref[:, here]
            for k in range(count):
                totals[k] = totals[k] + hid_ref[first + k : first + k + 1, here] * x
        for k in range(count):
            at = (first + k) * fields
            inner_ref[at : at + fields, :] = totals[k].astype(BF16)

    group, first = 4, 0
    products(0)
    for number in range(len(steps)):
        if number + 1 < len(steps):
            products(number + 1)
        if number % 3 == 0 and first < maps:
            inner(first, group)
            first += group
        sums(number)
    for first in range(first, maps, group):
        inner(first, group)
    base = fields * maps
    second = dot_lanes(up, inner_ref[...])
    for h in range(maps):
        grad_ref[base + h * maps : base + (h + 1) * maps, :] = second[:, h * fields : (h + 1) * fields]
    two = dot(second_ref[...], inner_ref[...])
    pooled = jnp.concatenate([one_ref[...], two], axis=0) * scale
    if not packed:
        outs[0][...] = grad_ref[...] * scales[1]
        outs[1][...] = pooled
        return
    cols, tabs = packed
    share = lanes // cols
    tall = 2 * maps * share // lanes
    for c in range(cols):
        pack_ref[c] = jnp.concatenate(
            [
                pooled[g * tall : (g + 1) * tall, c * share : (c + 1) * share]
                for g in range(lanes // share)
            ],
            axis=1,
        )
    own_col = place_ref[0]
    block = maps + maps // 2
    rows = tabs * block + tall
    for r in range(cols):
        c = jnp.bitwise_xor(own_col, r)
        out, base = outs[r % 2], r // 2 * rows
        for q in range(tabs):
            k = q * cols + c
            first = grad_ref[pl.ds(pl.multiple_of(k * 2 * maps, 2 * maps), 2 * maps), :]
            first = jnp.concatenate([first[:maps], first[maps:]], axis=1)
            second = grad_ref[pl.ds(pl.multiple_of((2 * tabs * cols + k) * maps, maps), maps), :]
            second = jnp.concatenate([second[: maps // 2], second[maps // 2 :]], axis=1)
            out[base + q * block : base + (q + 1) * block, :] = (
                jnp.concatenate([first, second], axis=0) * scales[1]
            ).astype(BF16)
        out[base + tabs * block : base + rows, :] = pack_ref[c].astype(BF16)


def filter_part(packed, scales, place, cot, second, embed, hidden, lower, one):
    fields, positions = embed.shape
    maps = hidden.shape[0]
    lanes = cot.shape[1]
    pair = 2 * lanes
    grads = (fields + maps) * maps
    if packed:
        cols, tabs = packed
        tall = 2 * maps // cols
        piece = (cols // 2 * (tabs * (maps + maps // 2) + tall), lanes)
        outs = [jax.ShapeDtypeStruct(piece, BF16)] * 2
        pack = pltpu.VMEM((cols, tall, lanes), F32)
    else:
        outs = [
            jax.ShapeDtypeStruct((grads, fields), F32),
            jax.ShapeDtypeStruct((2 * maps, lanes), F32),
        ]
        pack = pltpu.VMEM((1, 8, lanes), F32)
    return pl.pallas_call(
        functools.partial(filter_kernel, packed, scales),
        in_specs=[pl.BlockSpec(memory_space=pltpu.SMEM)] + [whole()] * 6,
        out_specs=[whole()] * len(outs),
        out_shape=outs,
        scratch_shapes=[
            pltpu.VMEM((fields, positions), F32),
            pltpu.VMEM((maps, positions), F32),
            pltpu.VMEM((maps * fields, lanes), BF16),
            pltpu.VMEM((grads, fields), F32),
            pltpu.VMEM((2, 512, pair), BF16),
            pack,
        ],
        compiler_params=params(),
        cost_estimate=cost(6 * maps * fields * fields * positions, 8 * embed.size),
        name="filter_part",
    )(place, cot, second, embed, hidden, lower, one)


def owner_kernel(table_ref, out_ref):
    width, slots, _ = out_ref.shape
    tabs, _, lanes = table_ref.shape
    for t in range(tabs):
        for d in range(width):
            out_ref[d, :, t * lanes : (t + 1) * lanes] = table_ref[t, d * slots : (d + 1) * slots, :]


def owner_part(table, slots, width):
    tabs, _, lanes = table.shape
    return pl.pallas_call(
        owner_kernel,
        in_specs=[whole()],
        out_specs=whole(),
        out_shape=jax.ShapeDtypeStruct((width, slots, tabs * lanes), BF16),
        compiler_params=params(),
        name="owner_part",
    )(table).transpose(1, 0, 2)


def grad_kernel(count, *refs):
    parts, (one_ref, two_ref) = refs[:count], refs[count:]
    maps, lanes = one_ref.shape
    blocks = [part[...] for part in parts] if count > 1 else [parts[0][t] for t in range(parts[0].shape[0])]
    total = functools.reduce(lambda a, b: a + b, [block.astype(F32) for block in blocks])
    one_ref[...] = total[:maps]
    two_ref[: maps // 2, :] = total[maps:, : lanes // 2]
    two_ref[maps // 2 :, :] = total[maps:, lanes // 2 :]


def grad_part(parts, maps):
    parts = parts if isinstance(parts, list) else [parts]
    lanes = parts[0].shape[-1]
    return pl.pallas_call(
        functools.partial(grad_kernel, len(parts)),
        in_specs=[whole()] * len(parts),
        out_specs=[whole()] * 2,
        out_shape=[
            jax.ShapeDtypeStruct((maps, lanes), F32),
            jax.ShapeDtypeStruct((maps, lanes // 2), F32),
        ],
        compiler_params=params(),
        name="grad_part",
    )(*parts)


def per_device(bag_items, lengths, field_slot, filter_one, filter_two, cotangent):
    slots, _, width, samples = bag_items.shape
    tabs = lax.axis_size("tab")
    cols = lax.axis_size("col")
    devices = tabs * cols
    lanes = samples // tabs
    maps = filter_one.shape[0]
    fields = field_slot.shape[0]
    scale = (width * cols) ** -0.5
    scales = (scale, samples**-0.5)
    sent = pool(bag_items, lengths, tabs)
    received = lax.all_to_all(sent, "tab", split_axis=0, concat_axis=0, tiled=True)
    cot = lax.all_gather(cotangent, "col", axis=1, tiled=True)
    square = filter_one.reshape(maps, fields, fields).astype(F32)
    sym = (square + square.transpose(0, 2, 1)).astype(BF16).reshape(maps * fields, fields)
    second = filter_two.reshape(maps * maps, fields)
    upper = (cot[maps:].astype(F32) * scale).astype(BF16)
    inner = lax.dot_general(
        filter_two, upper, (((0,), (0,)), ((), ())), preferred_element_type=F32
    ).astype(BF16).astype(F32)
    small = slots % 16 != 0
    if small:
        received = received.reshape(tabs, width, slots, lanes).transpose(1, 0, 2, 3)
        received = received.reshape(1, width * tabs * slots, lanes)
    packable = (
        fields * fields == devices * lanes
        and fields * 2 == lanes
        and maps == devices
        and cols & (cols - 1) == 0
        and cols > 1
        and tabs & (tabs - 1) == 0
        and not small
    )
    place = lax.axis_index("col").astype(jnp.int32).reshape(1)
    table, embed, hidden, lower, one = embed_part(
        scale, received, field_slot, cot, sym, second, inner, width
    )
    results = filter_part(
        (cols, tabs) if packable else None, scales, place, cot, filter_two, embed, hidden, lower, one
    )
    if small:
        table = table.reshape(width, tabs, slots, lanes).transpose(1, 0, 2, 3)
        table = table.reshape(tabs, width * slots, lanes)
    returned = lax.all_to_all(table, "tab", split_axis=0, concat_axis=0, tiled=True)
    if packable:
        block = maps + maps // 2
        def swap(value, bit, pieces):
            step = value.shape[0] // pieces
            moved = [
                lax.ppermute(
                    value[i * step : (i + 1) * step], "col", [(c, c ^ bit) for c in range(cols)]
                )
                for i in range(pieces)
            ]
            return jnp.concatenate(moved, axis=0) if pieces > 1 else moved[0]

        total = results[0].astype(F32) + swap(results[1], 1, 2).astype(F32)
        half = total.shape[0] // 2
        total = total[:half] + swap(total[half:].astype(BF16), 2, 1).astype(F32)
        grads = total[: tabs * block].astype(BF16).reshape(tabs, block, lanes)
        returned, grads = lax.optimization_barrier((returned, grads))
        grads = lax.all_to_all(grads, "tab", split_axis=0, concat_axis=0, tiled=True)
        pooled_grad = owner_part(returned, slots, width)
        grad_one, grad_two = grad_part(grads, maps)
        share = lanes // cols
        packs = total[tabs * block :]
        pooled = jnp.concatenate(
            [packs[:, g * share : (g + 1) * share] for g in range(lanes // share)], axis=0
        )
        return (pooled, grad_one, grad_two, pooled_grad)
    pooled_grad = owner_part(returned, slots, width)
    pooled = lax.psum_scatter(results[1], "col", scatter_dimension=1, tiled=True)
    shaped = results[0].reshape(fields + maps, maps, fields).transpose(1, 0, 2)
    grad_one = shaped[:, :fields].reshape(maps, tabs, cols, -1)
    grad_two = shaped[:, fields:].reshape(maps, tabs, cols, -1)
    grad_one = lax.psum_scatter(grad_one, "col", scatter_dimension=2, tiled=True)
    grad_two = lax.psum_scatter(grad_two, "col", scatter_dimension=2, tiled=True)
    grad_one = lax.psum_scatter(grad_one, "tab", scatter_dimension=1, tiled=True)
    grad_two = lax.psum_scatter(grad_two, "tab", scatter_dimension=1, tiled=True)
    return (pooled, grad_one.reshape(maps, -1), grad_two.reshape(maps, -1), pooled_grad)


def solution(mesh):
    in_specs = (P("tab", None, "col", None), P("tab", None), P(), P(), P(), P(None, ("tab", "col")))
    out_specs = (
        P(None, ("tab", "col")),
        P(None, ("tab", "col")),
        P(None, ("tab", "col")),
        P("tab", "col", None),
    )
    return jax.shard_map(
        per_device, mesh=mesh, in_specs=in_specs, out_specs=out_specs, check_vma=False
    )
```

```python
import functools

import jax
import jax.numpy as jnp
from jax import lax
from jax.experimental import pallas as pl
from jax.experimental.pallas import tpu as pltpu
from jax.sharding import PartitionSpec as P

BF16 = jnp.bfloat16
F32 = jnp.float32
VMEM_BYTES = 48 * 1024 * 1024
MATMUL_ROWS = 1024
FILTER_ROWS = 512


def params():
    return pltpu.CompilerParams(vmem_limit_bytes=VMEM_BYTES)


def cost(flops, moved):
    return pl.CostEstimate(flops=flops, bytes_accessed=moved, transcendentals=0)


def whole():
    return pl.BlockSpec(memory_space=pltpu.VMEM)


def dot(left, right):
    return jnp.dot(left, right, preferred_element_type=F32)


def dot_lanes(left, right):
    return lax.dot_general(left, right, (((1,), (1,)), ((), ())), preferred_element_type=F32)


def tab_orders(tabs):
    first = [t // 2 if t % 2 == 0 else tabs - 1 - t // 2 for t in range(tabs)]
    return first, first[tabs // 2 :] + first[: tabs // 2]


def position(orders, place_ref, t):
    near, far = orders[0].index(t), orders[1].index(t)
    if near == far:
        return near
    return jnp.where(lax.rem(place_ref[0], 2) == 0, near, far)


def exchange(value, orders, cols):
    if orders[0] == orders[1]:
        return lax.all_to_all(value, "tab", split_axis=0, concat_axis=0, tiled=True)
    groups = [[t * cols + c for t in orders[c % 2]] for c in range(cols)]
    return lax.all_to_all(
        value, ("tab", "col"), split_axis=0, concat_axis=0, tiled=True, axis_index_groups=groups
    )


def pool_kernel(steps, orders, place_ref, bag_hbm, lengths_hbm, out_ref, bag_ref, lengths_ref, rows_ref, sems):
    slots, width, items, _ = bag_hbm.shape
    chunks, _, lanes = out_ref.shape
    per_step = chunks // steps
    counts = pltpu.make_async_copy(lengths_hbm, lengths_ref, sems.at[steps])
    counts.start()
    copies = []
    for k in range(steps):
        part = pl.ds(k * per_step * lanes, per_step * lanes)
        copy = pltpu.make_async_copy(
            bag_hbm.at[:, :, :, part], bag_ref.at[:, :, :, part], sems.at[k]
        )
        copy.start()
        copies.append(copy)
    counts.wait()
    for chunk in range(chunks):
        if chunk % per_step == 0:
            copies[chunk // per_step].wait()
        here = pl.ds(chunk * lanes, lanes)
        buffer = chunk % 2
        block = position(orders, place_ref, chunk)
        for slot in range(slots):
            at = slot * width * items
            rows_ref[buffer, at : at + width * items, :] = (
                bag_ref[slot, :, :, here].astype(F32).reshape(width * items, lanes)
            )
        count = lengths_ref[:, here]
        for d in range(width):
            total = jnp.zeros((slots, lanes), F32)
            for item in range(items):
                value = rows_ref[buffer, pl.ds(d * items + item, slots, stride=width * items), :]
                total = total + jnp.where(count > item, value, 0.0)
            out_ref[block, d * slots : (d + 1) * slots, :] = total.astype(BF16)


def pool(orders, place, bag_items, lengths):
    tab_count = len(orders[0])
    bag = bag_items.transpose(0, 2, 1, 3)
    slots, width, items, samples = bag.shape
    lanes = samples // tab_count
    steps = min(4, tab_count)
    return pl.pallas_call(
        functools.partial(pool_kernel, steps, orders),
        in_specs=[pl.BlockSpec(memory_space=pltpu.SMEM)] + [pl.BlockSpec(memory_space=pltpu.HBM)] * 2,
        out_specs=whole(),
        out_shape=jax.ShapeDtypeStruct((tab_count, width * slots, lanes), BF16),
        scratch_shapes=[
            pltpu.VMEM(bag.shape, BF16),
            pltpu.VMEM(lengths.shape, jnp.int32),
            pltpu.VMEM((2, width * slots * items, lanes), F32),
            pltpu.SemaphoreType.DMA((steps + 1,)),
        ],
        compiler_params=pltpu.CompilerParams(vmem_limit_bytes=62 * 1024 * 1024),
        name="pool_bags",
    )(place, bag, lengths)


def forward_kernel(
    packed, orders, scales, count,
    place_ref, received_ref, slot_ref, sym_ref, second_ref, filter_ref,
    *refs,
):
    cot_refs, refs = refs[:count], refs[count:]
    outs = refs[:2]
    (
        embed_ref, hidden_ref, lower_ref, upper_ref,
        cot_ref, up_ref, x_ref, hid_ref, maps_ref, sum_ref, inner_ref, grad_ref, buf_ref, pair_ref,
        pack_ref,
    ) = refs[2:]
    fields = slot_ref.shape[0]
    maps, positions = hidden_ref.shape
    lanes = upper_ref.shape[1]
    width = positions // lanes
    tabs = received_ref.shape[0]
    slots = received_ref.shape[1] // width
    pair = 2 * lanes
    scale = scales[0]
    for r in range(count):
        cot_ref[r] = cot_refs[r][...].astype(F32)
    share = lanes // count
    for c in range(count):
        block = cot_ref[jnp.bitwise_xor(place_ref[0], c)] if count > 1 else cot_ref[0]
        up_ref[:, c * share : (c + 1) * share] = (block * scale).astype(BF16).astype(F32)
    up_ref[:, lanes:] = up_ref[:, :lanes]
    upper = up_ref[maps:, :lanes].astype(BF16)
    upper_ref[...] = upper
    onehot = (
        lax.broadcasted_iota(jnp.int32, (fields, tabs * slots), 1) == slot_ref[...]
    ).astype(BF16)
    order = [position(orders, place_ref, t) if tabs > 1 else 0 for t in range(tabs)]
    for d in range(width):
        parts = [received_ref[order[t], d * slots : (d + 1) * slots, :] for t in range(tabs)]
        x = dot(onehot, parts[0] if len(parts) == 1 else jnp.concatenate(parts, axis=0))
        x_ref[:, d * lanes : (d + 1) * lanes] = x
        embed_ref[:, d * lanes : (d + 1) * lanes] = x.astype(BF16)
    sum_ref[...] = jnp.zeros_like(sum_ref)
    rows = MATMUL_ROWS
    jobs = []
    for p in range(width // 2):
        jobs += [("z", p, start) for start in range(0, maps * maps, rows)]
        jobs += [("y", p, start) for start in range(0, maps * fields, rows)]

    def issue(number):
        kind, p, start = jobs[number]
        source = second_ref if kind == "z" else sym_ref
        x = embed_ref[:, p * pair : (p + 1) * pair]
        buf_ref[number % 2] = dot(source[start : start + rows, :], x)

    state = {}

    def consume(number):
        kind, p, start = jobs[number]
        here = pl.ds(p * pair, pair)
        b = p % 2
        y_ref = buf_ref.at[number % 2]
        if kind == "z":
            lower = up_ref[:maps, :] if start == 0 else state["lower"]
            for k in range(rows // maps):
                o = start // maps + k
                lower = lower + up_ref[maps + o : maps + o + 1, :] * y_ref[k * maps : (k + 1) * maps, :]
            state["lower"] = lower
            if start + rows == maps * maps:
                lower_ref[:, here] = lower.astype(BF16)
            return
        x_float = x_ref[:, here]
        for k in range(rows // fields):
            o = start // fields + k
            mine = y_ref[k * fields : (k + 1) * fields, :]
            maps_ref[b, o : o + 1, :] = 0.5 * jnp.sum(mine * x_float, axis=0, keepdims=True)
        if start + rows < maps * fields:
            return
        first_maps = maps_ref[b]
        sum_ref[...] += first_maps
        hidden = first_maps.astype(BF16)
        hidden_ref[:, here] = hidden
        hid_ref[:, here] = hidden.astype(F32)

    issue(0)
    for number in range(len(jobs)):
        if number + 1 < len(jobs):
            issue(number + 1)
        consume(number)

    rows = FILTER_ROWS
    steps = [
        (p, start) for p in range(width // 2) for start in range(0, fields * maps, rows)
    ]

    def products(number):
        p, start = steps[number]
        here = pl.ds(p * pair, pair)
        lower = lower_ref[:, here].astype(F32)
        for k in range(rows // maps):
            f = start // maps + k
            pair_ref[number % 2, k * maps : (k + 1) * maps, :] = (
                x_ref[f : f + 1, here] * lower
            ).astype(BF16)

    def sums(number):
        p, start = steps[number]
        part = dot_lanes(pair_ref[number % 2], embed_ref[:, p * pair : (p + 1) * pair])
        if p == 0:
            grad_ref[start : start + rows, :] = part
        else:
            grad_ref[start : start + rows, :] += part

    def inner(first, size):
        totals = [jnp.zeros((fields, lanes), F32)] * size
        for d in range(width):
            here = pl.ds(d * lanes, lanes)
            x = x_ref[:, here]
            for k in range(size):
                totals[k] = totals[k] + hid_ref[first + k : first + k + 1, here] * x
        for k in range(size):
            at = (first + k) * fields
            inner_ref[at : at + fields, :] = totals[k].astype(BF16)

    group, first = 4, 0
    products(0)
    for number in range(len(steps)):
        if number + 1 < len(steps):
            products(number + 1)
        if number % 3 == 0 and first < maps:
            inner(first, group)
            first += group
        sums(number)
    for first in range(first, maps, group):
        inner(first, group)
    base = fields * maps
    second = dot_lanes(upper, inner_ref[...])
    for h in range(maps):
        grad_ref[base + h * maps : base + (h + 1) * maps, :] = second[:, h * fields : (h + 1) * fields]
    two = dot(filter_ref[...], inner_ref[...])
    pooled = jnp.concatenate([sum_ref[:, :lanes] + sum_ref[:, lanes:], two], axis=0) * scale
    if not packed:
        outs[0][...] = grad_ref[...] * scales[1]
        outs[1][...] = pooled
        return
    cols, tabs = packed
    tall = 2 * maps * share // lanes
    for c in range(cols):
        pack_ref[c] = jnp.concatenate(
            [
                pooled[g * tall : (g + 1) * tall, c * share : (c + 1) * share]
                for g in range(lanes // share)
            ],
            axis=1,
        )
    own_col = place_ref[0]
    block = maps + maps // 2
    rows = tabs * block + tall
    for r in range(cols):
        c = jnp.bitwise_xor(own_col, r)
        out, base = outs[r % 2], r // 2 * rows
        for q in range(tabs):
            near, far = orders[0][q], orders[1][q]
            k = jnp.where(lax.rem(c, 2) == 0, near, far) * cols + c
            first = grad_ref[pl.ds(pl.multiple_of(k * 2 * maps, 2 * maps), 2 * maps), :]
            first = jnp.concatenate([first[:maps], first[maps:]], axis=1)
            second = grad_ref[pl.ds(pl.multiple_of((2 * tabs * cols + k) * maps, maps), maps), :]
            second = jnp.concatenate([second[: maps // 2], second[maps // 2 :]], axis=1)
            out[base + q * block : base + (q + 1) * block, :] = (
                jnp.concatenate([first, second], axis=0) * scales[1]
            ).astype(BF16)
        out[base + tabs * block : base + rows, :] = pack_ref[c].astype(BF16)


def forward_part(packed, orders, scales, place, received, slot, cots, sym, second, filter_two, width):
    fields = slot.shape[0]
    maps = cots[0].shape[0] // 2
    lanes = cots[0].shape[1] * len(cots)
    positions = width * lanes
    pair = 2 * lanes
    grads = (fields + maps) * maps
    if packed:
        cols, tabs = packed
        tall = 2 * maps // cols
        piece = (cols // 2 * (tabs * (maps + maps // 2) + tall), lanes)
        outs = [jax.ShapeDtypeStruct(piece, BF16)] * 2
        pack = pltpu.VMEM((cols, tall, lanes), F32)
    else:
        outs = [
            jax.ShapeDtypeStruct((grads, fields), F32),
            jax.ShapeDtypeStruct((2 * maps, lanes), F32),
        ]
        pack = pltpu.VMEM((1, 8, lanes), F32)
    return pl.pallas_call(
        functools.partial(forward_kernel, packed, orders, scales, len(cots)),
        in_specs=[pl.BlockSpec(memory_space=pltpu.SMEM)] + [whole()] * (5 + len(cots)),
        out_specs=[whole()] * 6,
        out_shape=outs
        + [
            jax.ShapeDtypeStruct((fields, positions), BF16),
            jax.ShapeDtypeStruct((maps, positions), BF16),
            jax.ShapeDtypeStruct((maps, positions), BF16),
            jax.ShapeDtypeStruct((maps, lanes), BF16),
        ],
        scratch_shapes=[
            pltpu.VMEM((len(cots),) + cots[0].shape, F32),
            pltpu.VMEM((2 * maps, pair), F32),
            pltpu.VMEM((fields, positions), F32),
            pltpu.VMEM((maps, positions), F32),
            pltpu.VMEM((2, maps, pair), F32),
            pltpu.VMEM((maps, pair), F32),
            pltpu.VMEM((maps * fields, lanes), BF16),
            pltpu.VMEM((grads, fields), F32),
            pltpu.VMEM((2, MATMUL_ROWS, pair), F32),
            pltpu.VMEM((2, FILTER_ROWS, pair), BF16),
            pack,
        ],
        compiler_params=params(),
        cost_estimate=cost(8 * maps * fields * fields * positions, 4 * received.size),
        name="forward_part",
    )(place, received, slot.reshape(fields, 1), sym, second, filter_two, *cots)


def embed_kernel(
    orders, slots,
    place_ref, slot_ref, sym_ref, turned_ref, upper_ref, embed_ref, hidden_ref, lower_ref,
    table_ref, inner_ref, low_ref, hid_ref, buf_ref,
):
    fields, positions = embed_ref.shape
    maps, lanes = upper_ref.shape
    width = positions // lanes
    tabs = table_ref.shape[0]
    pair = 2 * lanes
    spread = (
        lax.broadcasted_iota(jnp.int32, (tabs * slots, fields), 0) == slot_ref[...]
    ).astype(BF16)
    order = [position(orders, place_ref, t) if tabs > 1 else 0 for t in range(tabs)]
    inner_ref[...] = dot(turned_ref[...], upper_ref[...])
    low_ref[...] = lower_ref[...].astype(F32)
    hid_ref[...] = hidden_ref[...].astype(F32)
    rows = MATMUL_ROWS
    jobs = [(p, start) for p in range(width // 2) for start in range(0, maps * fields, rows)]

    def issue(number):
        p, start = jobs[number]
        x = embed_ref[:, p * pair : (p + 1) * pair]
        buf_ref[number % 2] = dot(sym_ref[start : start + rows, :], x)

    state = {}

    def consume(number):
        p, start = jobs[number]
        here = pl.ds(p * pair, pair)
        y_ref = buf_ref.at[number % 2]
        gradient = jnp.zeros((fields, pair), F32) if start == 0 else state["gradient"]
        for k in range(rows // fields):
            o = start // fields + k
            gradient = gradient + low_ref[o : o + 1, here] * y_ref[k * fields : (k + 1) * fields, :]
        state["gradient"] = gradient
        if start + rows < maps * fields:
            return
        sides = [gradient[:, :lanes], gradient[:, lanes:]]
        for h in range(maps):
            inner = inner_ref[h * fields : (h + 1) * fields, :]
            for k in range(2):
                at = pl.ds(p * pair + k * lanes, lanes)
                sides[k] = sides[k] + hid_ref[h : h + 1, at] * inner
        for k in range(2):
            table = dot(spread, sides[k].astype(BF16)).astype(BF16)
            at = (2 * p + k) * slots
            for t in range(tabs):
                table_ref[order[t], at : at + slots, :] = table[t * slots : (t + 1) * slots, :]

    issue(0)
    for number in range(len(jobs)):
        if number + 1 < len(jobs):
            issue(number + 1)
        consume(number)


def embed_part(orders, slots, place, slot, sym, turned, upper, embed, hidden, lower, shape):
    fields, positions = embed.shape
    maps, lanes = upper.shape
    pair = 2 * lanes
    return pl.pallas_call(
        functools.partial(embed_kernel, orders, slots),
        in_specs=[pl.BlockSpec(memory_space=pltpu.SMEM)] + [whole()] * 7,
        out_specs=whole(),
        out_shape=jax.ShapeDtypeStruct(shape, BF16),
        scratch_shapes=[
            pltpu.VMEM((maps * fields, lanes), F32),
            pltpu.VMEM((maps, positions), F32),
            pltpu.VMEM((maps, positions), F32),
            pltpu.VMEM((2, MATMUL_ROWS, pair), F32),
        ],
        compiler_params=params(),
        cost_estimate=cost(4 * maps * fields * fields * positions, 8 * embed.size),
        name="embed_part",
    )(place, slot.reshape(1, fields), sym, turned, upper, embed, hidden, lower)


def owner_kernel(orders, place_ref, table_ref, out_ref, *grads):
    width, slots, _ = out_ref.shape
    tabs, _, lanes = table_ref.shape
    for t in range(tabs):
        block = position(orders, place_ref, t)
        for d in range(width):
            out_ref[d, :, t * lanes : (t + 1) * lanes] = table_ref[
                block, d * slots : (d + 1) * slots, :
            ]
    if not grads:
        return
    one_ref, two_ref = grads
    maps = one_ref.shape[0]
    total = table_ref[0, width * slots :, :].astype(F32)
    for t in range(1, tabs):
        total = total + table_ref[t, width * slots :, :].astype(F32)
    one_ref[...] = total[:maps]
    two_ref[: maps // 2, :] = total[maps:, : lanes // 2]
    two_ref[maps // 2 :, :] = total[maps:, lanes // 2 :]


def owner_part(orders, place, table, slots, width, maps):
    tabs, rows, lanes = table.shape
    shapes = [jax.ShapeDtypeStruct((width, slots, tabs * lanes), BF16)]
    if rows > width * slots:
        shapes += [
            jax.ShapeDtypeStruct((maps, lanes), F32),
            jax.ShapeDtypeStruct((maps, lanes // 2), F32),
        ]
    results = pl.pallas_call(
        functools.partial(owner_kernel, orders),
        in_specs=[pl.BlockSpec(memory_space=pltpu.SMEM), whole()],
        out_specs=[whole()] * len(shapes),
        out_shape=shapes,
        compiler_params=params(),
        name="owner_part",
    )(place, table)
    return results[0].transpose(1, 0, 2), *results[1:]


def per_device(bag_items, lengths, field_slot, filter_one, filter_two, cotangent):
    slots, _, width, samples = bag_items.shape
    tabs = lax.axis_size("tab")
    cols = lax.axis_size("col")
    devices = tabs * cols
    lanes = samples // tabs
    maps = filter_one.shape[0]
    fields = field_slot.shape[0]
    scales = ((width * cols) ** -0.5, samples**-0.5)
    place = lax.axis_index("col").astype(jnp.int32).reshape(1)
    small = slots % 16 != 0
    packable = (
        fields * fields == devices * lanes
        and fields * 2 == lanes
        and maps == devices
        and cols & (cols - 1) == 0
        and cols > 1
        and tabs % 2 == 0
        and not small
    )
    orders = tab_orders(tabs) if packable else (list(range(tabs)),) * 2
    sent = pool(orders, place, bag_items, lengths)
    sent, cotangent = lax.optimization_barrier((sent, cotangent))
    received = exchange(sent, orders, cols)
    if cols & (cols - 1):
        cots = [lax.all_gather(cotangent, "col", axis=1, tiled=True)]
    else:
        cots = [cotangent] + [
            lax.ppermute(cotangent, "col", [(c, c ^ r) for c in range(cols)])
            for r in range(1, cols)
        ]
    square = filter_one.reshape(maps, fields, fields).astype(F32)
    sym = (square + square.transpose(0, 2, 1)).astype(BF16).reshape(maps * fields, fields)
    second = filter_two.reshape(maps * maps, fields)
    if small:
        received = received.reshape(tabs, width, slots, lanes).transpose(1, 0, 2, 3)
        received = received.reshape(1, width * tabs * slots, lanes)
    keep, away, embed, hidden, lower, upper = forward_part(
        (cols, tabs) if packable else None,
        orders, scales, place, received, field_slot, cots, sym, second, filter_two, width,
    )
    chunks, rows, _ = received.shape
    block = maps + maps // 2 if packable else 0
    table = embed_part(
        orders, rows // width, place, field_slot, sym, filter_two.T, upper, embed, hidden, lower,
        (chunks, rows + block, lanes),
    )
    if packable:
        total = keep.astype(F32)
        bit = 1
        while True:
            total = total + lax.ppermute(
                away, "col", [(c, c ^ bit) for c in range(cols)]
            ).astype(F32)
            bit *= 2
            if bit == cols:
                break
            half = total.shape[0] // 2
            total, away = total[:half], total[half:].astype(BF16)
        grads = total[: tabs * block].astype(BF16).reshape(tabs, block, lanes)
        table = lax.dynamic_update_slice(table, grads, (0, rows, 0))
        returned = exchange(table, orders, cols)
        pooled_grad, grad_one, grad_two = owner_part(orders, place, returned, slots, width, maps)
        share = lanes // cols
        packs = total[tabs * block :]
        pooled = jnp.concatenate(
            [packs[:, g * share : (g + 1) * share] for g in range(lanes // share)], axis=0
        )
        return (pooled, grad_one, grad_two, pooled_grad)
    if small:
        table = table.reshape(width, tabs, slots, lanes).transpose(1, 0, 2, 3)
        table = table.reshape(tabs, width * slots, lanes)
    returned = exchange(table, orders, cols)
    (pooled_grad,) = owner_part(orders, place, returned, slots, width, maps)
    pooled = lax.psum_scatter(away, "col", scatter_dimension=1, tiled=True)
    shaped = keep.reshape(fields + maps, maps, fields).transpose(1, 0, 2)
    grad_one = shaped[:, :fields].reshape(maps, tabs, cols, -1)
    grad_two = shaped[:, fields:].reshape(maps, tabs, cols, -1)
    grad_one = lax.psum_scatter(grad_one, "col", scatter_dimension=2, tiled=True)
    grad_two = lax.psum_scatter(grad_two, "col", scatter_dimension=2, tiled=True)
    grad_one = lax.psum_scatter(grad_one, "tab", scatter_dimension=1, tiled=True)
    grad_two = lax.psum_scatter(grad_two, "tab", scatter_dimension=1, tiled=True)
    return (pooled, grad_one.reshape(maps, -1), grad_two.reshape(maps, -1), pooled_grad)


def solution(mesh):
    in_specs = (P("tab", None, "col", None), P("tab", None), P(), P(), P(), P(None, ("tab", "col")))
    out_specs = (
        P(None, ("tab", "col")),
        P(None, ("tab", "col")),
        P(None, ("tab", "col")),
        P("tab", "col", None),
    )
    return jax.shard_map(
        per_device, mesh=mesh, in_specs=in_specs, out_specs=out_specs, check_vma=False
    )
```

```python
import functools

import jax
import jax.numpy as jnp
from jax import lax
from jax.experimental import pallas as pl
from jax.experimental.pallas import tpu as pltpu
from jax.sharding import PartitionSpec as P

BF16 = jnp.bfloat16
F32 = jnp.float32
VMEM_BYTES = 48 * 1024 * 1024
MATMUL_ROWS = 1024
FILTER_ROWS = 512
INNER_GROUPS = 2


def params():
    return pltpu.CompilerParams(vmem_limit_bytes=VMEM_BYTES)


def cost(flops, moved):
    return pl.CostEstimate(flops=flops, bytes_accessed=moved, transcendentals=0)


def whole():
    return pl.BlockSpec(memory_space=pltpu.VMEM)


def dot(left, right):
    return jnp.dot(left, right, preferred_element_type=F32)


def dot_lanes(left, right):
    return lax.dot_general(left, right, (((1,), (1,)), ((), ())), preferred_element_type=F32)


def tab_orders(tabs):
    first = [tabs - 1 - i // 2 if i % 2 == 0 else i // 2 for i in range(tabs)]
    return first, first[tabs // 2 :] + first[: tabs // 2]


def position(orders, place_ref, t):
    near, far = orders[0].index(t), orders[1].index(t)
    if near == far:
        return near
    return jnp.where(lax.rem(place_ref[0], 2) == 0, near, far)


def exchange(value, orders, cols):
    if orders[0] == orders[1]:
        return lax.all_to_all(value, "tab", split_axis=0, concat_axis=0, tiled=True)
    groups = [[t * cols + c for t in orders[c % 2]] for c in range(cols)]
    return lax.all_to_all(
        value, ("tab", "col"), split_axis=0, concat_axis=0, tiled=True, axis_index_groups=groups
    )


def pool_kernel(steps, orders, place_ref, bag_hbm, lengths_hbm, out_ref, bag_ref, lengths_ref, rows_ref, sems):
    slots, width, items, _ = bag_hbm.shape
    chunks, _, lanes = out_ref.shape
    per_step = chunks // steps
    counts = pltpu.make_async_copy(lengths_hbm, lengths_ref, sems.at[steps])
    counts.start()
    copies = []
    for k in range(steps):
        part = pl.ds(k * per_step * lanes, per_step * lanes)
        copy = pltpu.make_async_copy(
            bag_hbm.at[:, :, :, part], bag_ref.at[:, :, :, part], sems.at[k]
        )
        copy.start()
        copies.append(copy)
    counts.wait()
    for chunk in range(chunks):
        if chunk % per_step == 0:
            copies[chunk // per_step].wait()
        here = pl.ds(chunk * lanes, lanes)
        buffer = chunk % 2
        block = position(orders, place_ref, chunk)
        for slot in range(slots):
            at = slot * width * items
            rows_ref[buffer, at : at + width * items, :] = (
                bag_ref[slot, :, :, here].astype(F32).reshape(width * items, lanes)
            )
        count = lengths_ref[:, here]
        for d in range(width):
            total = jnp.zeros((slots, lanes), F32)
            for item in range(items):
                value = rows_ref[buffer, pl.ds(d * items + item, slots, stride=width * items), :]
                total = total + jnp.where(count > item, value, 0.0)
            out_ref[block, d * slots : (d + 1) * slots, :] = total.astype(BF16)


def pool(orders, place, bag_items, lengths):
    tab_count = len(orders[0])
    bag = bag_items.transpose(0, 2, 1, 3)
    slots, width, items, samples = bag.shape
    lanes = samples // tab_count
    steps = min(4, tab_count)
    return pl.pallas_call(
        functools.partial(pool_kernel, steps, orders),
        in_specs=[pl.BlockSpec(memory_space=pltpu.SMEM)] + [pl.BlockSpec(memory_space=pltpu.HBM)] * 2,
        out_specs=whole(),
        out_shape=jax.ShapeDtypeStruct((tab_count, width * slots, lanes), BF16),
        scratch_shapes=[
            pltpu.VMEM(bag.shape, BF16),
            pltpu.VMEM(lengths.shape, jnp.int32),
            pltpu.VMEM((2, width * slots * items, lanes), F32),
            pltpu.SemaphoreType.DMA((steps + 1,)),
        ],
        compiler_params=pltpu.CompilerParams(vmem_limit_bytes=62 * 1024 * 1024),
        name="pool_bags",
    )(place, bag, lengths)


def forward_kernel(
    packed, orders, scales, count,
    place_ref, received_ref, slot_ref, sym_ref, second_ref, filter_ref,
    *refs,
):
    cot_refs, refs = refs[:count], refs[count:]
    outs = refs[:2]
    (
        embed_ref, hidden_ref, lower_ref, upper_ref,
        cot_ref, up_ref, x_ref, hid_ref, maps_ref, sum_ref, inner_ref, grad_ref, buf_ref, pair_ref,
        pack_ref,
    ) = refs[2:]
    fields = slot_ref.shape[0]
    maps, positions = hidden_ref.shape
    lanes = upper_ref.shape[1]
    width = positions // lanes
    tabs = received_ref.shape[0]
    slots = received_ref.shape[1] // width
    pair = 2 * lanes
    scale = scales[0]
    for r in range(count):
        cot_ref[r] = cot_refs[r][...].astype(F32)
    share = lanes // count
    for c in range(count):
        block = cot_ref[jnp.bitwise_xor(place_ref[0], c)] if count > 1 else cot_ref[0]
        up_ref[:, c * share : (c + 1) * share] = (block * scale).astype(BF16).astype(F32)
    up_ref[:, lanes:] = up_ref[:, :lanes]
    upper = up_ref[maps:, :lanes].astype(BF16)
    upper_ref[...] = upper
    onehot = (
        lax.broadcasted_iota(jnp.int32, (fields, tabs * slots), 1) == slot_ref[...]
    ).astype(BF16)
    order = [position(orders, place_ref, t) if tabs > 1 else 0 for t in range(tabs)]
    for d in range(width):
        parts = [received_ref[order[t], d * slots : (d + 1) * slots, :] for t in range(tabs)]
        x = dot(onehot, parts[0] if len(parts) == 1 else jnp.concatenate(parts, axis=0))
        x_ref[:, d * lanes : (d + 1) * lanes] = x
        embed_ref[:, d * lanes : (d + 1) * lanes] = x.astype(BF16)
    sum_ref[...] = jnp.zeros_like(sum_ref)
    rows = MATMUL_ROWS
    jobs = []
    for p in range(width // 2):
        jobs += [("z", p, start) for start in range(0, maps * maps, rows)]
        jobs += [("y", p, start) for start in range(0, maps * fields, rows)]

    def issue(number):
        kind, p, start = jobs[number]
        source = second_ref if kind == "z" else sym_ref
        x = embed_ref[:, p * pair : (p + 1) * pair]
        buf_ref[number % 2] = dot(source[start : start + rows, :], x)

    state = {}

    def consume(number):
        kind, p, start = jobs[number]
        here = pl.ds(p * pair, pair)
        b = p % 2
        y_ref = buf_ref.at[number % 2]
        if kind == "z":
            lower = up_ref[:maps, :] if start == 0 else state["lower"]
            for k in range(rows // maps):
                o = start // maps + k
                lower = lower + up_ref[maps + o : maps + o + 1, :] * y_ref[k * maps : (k + 1) * maps, :]
            state["lower"] = lower
            if start + rows == maps * maps:
                lower_ref[:, here] = lower.astype(BF16)
            return
        x_float = x_ref[:, here]
        for k in range(rows // fields):
            o = start // fields + k
            mine = y_ref[k * fields : (k + 1) * fields, :]
            maps_ref[b, o : o + 1, :] = 0.5 * jnp.sum(mine * x_float, axis=0, keepdims=True)
        if start + rows < maps * fields:
            return
        first_maps = maps_ref[b]
        sum_ref[...] += first_maps
        hidden = first_maps.astype(BF16)
        hidden_ref[:, here] = hidden
        hid_ref[:, here] = hidden.astype(F32)

    issue(0)
    for number in range(len(jobs)):
        if number + 1 < len(jobs):
            issue(number + 1)
        consume(number)

    some = FILTER_ROWS // maps
    own_col = place_ref[0]

    def products(first):
        lower = lower_ref[...].astype(F32)
        for k in range(some):
            f = first + k
            pair_ref[first // some % 2, k * maps : (k + 1) * maps, :] = (
                x_ref[f : f + 1, :] * lower
            ).astype(BF16)

    def keep_rows(k, rows, at):
        cols, tabs = packed
        c = k % cols
        at += orders[c % 2].index(k // cols) * (maps + maps // 2)
        half = rows.shape[0] // 2
        both = jnp.concatenate([rows[:half], rows[half:]], axis=1) * scales[1]
        pack_ref[jnp.bitwise_xor(own_col, c), at : at + half, :] = both.astype(BF16)

    def sums(first):
        part = dot_lanes(pair_ref[first // some % 2], embed_ref[...])
        if not packed:
            grad_ref[first * maps : (first + some) * maps, :] = part
            return
        for k in range(some // 2):
            keep_rows(first // 2 + k, part[2 * k * maps : 2 * (k + 1) * maps], 0)

    def inner(first, size):
        totals = [jnp.zeros((fields, lanes), F32)] * size
        for d in range(width):
            here = pl.ds(d * lanes, lanes)
            x = x_ref[:, here]
            for k in range(size):
                totals[k] = totals[k] + hid_ref[first + k : first + k + 1, here] * x
        for k in range(size):
            at = (first + k) * fields
            inner_ref[at : at + fields, :] = totals[k].astype(BF16)

    group, done = 4, 0
    products(0)
    for first in range(0, fields, some):
        if first + some < fields:
            products(first + some)
        for _ in range(INNER_GROUPS):
            if done < maps:
                inner(done, group)
                done += group
        sums(first)
    for done in range(done, maps, group):
        inner(done, group)
    second = dot_lanes(upper, inner_ref[...])
    two = dot(filter_ref[...], inner_ref[...])
    pooled = jnp.concatenate([sum_ref[:, :lanes] + sum_ref[:, lanes:], two], axis=0) * scale
    if not packed:
        base = fields * maps
        for h in range(maps):
            grad_ref[base + h * maps : base + (h + 1) * maps, :] = second[
                :, h * fields : (h + 1) * fields
            ]
        outs[0][...] = grad_ref[...] * scales[1]
        outs[1][...] = pooled
        return
    cols, tabs = packed
    for h in range(maps):
        keep_rows(h, second[:, h * fields : (h + 1) * fields], maps)
    tall = 2 * maps * share // lanes
    last = tabs * (maps + maps // 2)
    for c in range(cols):
        pack_ref[jnp.bitwise_xor(own_col, c), last : last + tall, :] = jnp.concatenate(
            [
                pooled[g * tall : (g + 1) * tall, c * share : (c + 1) * share]
                for g in range(lanes // share)
            ],
            axis=1,
        ).astype(BF16)
    for r in range(cols):
        outs[r % 2][r // 2 * (last + tall) : (r // 2 + 1) * (last + tall), :] = pack_ref[r]


def forward_part(packed, orders, scales, place, received, slot, cots, sym, second, filter_two, width):
    fields = slot.shape[0]
    maps = cots[0].shape[0] // 2
    lanes = cots[0].shape[1] * len(cots)
    positions = width * lanes
    pair = 2 * lanes
    grads = (fields + maps) * maps
    if packed:
        cols, tabs = packed
        tall = 2 * maps // cols
        piece = (cols // 2 * (tabs * (maps + maps // 2) + tall), lanes)
        outs = [jax.ShapeDtypeStruct(piece, BF16)] * 2
        pack = pltpu.VMEM((cols, tabs * (maps + maps // 2) + tall, lanes), BF16)
    else:
        outs = [
            jax.ShapeDtypeStruct((grads, fields), F32),
            jax.ShapeDtypeStruct((2 * maps, lanes), F32),
        ]
        pack = pltpu.VMEM((1, 16, lanes), BF16)
    return pl.pallas_call(
        functools.partial(forward_kernel, packed, orders, scales, len(cots)),
        in_specs=[pl.BlockSpec(memory_space=pltpu.SMEM)] + [whole()] * (5 + len(cots)),
        out_specs=[whole()] * 6,
        out_shape=outs
        + [
            jax.ShapeDtypeStruct((fields, positions), BF16),
            jax.ShapeDtypeStruct((maps, positions), BF16),
            jax.ShapeDtypeStruct((maps, positions), BF16),
            jax.ShapeDtypeStruct((maps, lanes), BF16),
        ],
        scratch_shapes=[
            pltpu.VMEM((len(cots),) + cots[0].shape, F32),
            pltpu.VMEM((2 * maps, pair), F32),
            pltpu.VMEM((fields, positions), F32),
            pltpu.VMEM((maps, positions), F32),
            pltpu.VMEM((2, maps, pair), F32),
            pltpu.VMEM((maps, pair), F32),
            pltpu.VMEM((maps * fields, lanes), BF16),
            pltpu.VMEM((8 if packed else grads, fields), F32),
            pltpu.VMEM((2, MATMUL_ROWS, pair), F32),
            pltpu.VMEM((2, FILTER_ROWS, positions), BF16),
            pack,
        ],
        compiler_params=params(),
        cost_estimate=cost(8 * maps * fields * fields * positions, 4 * received.size),
        name="forward_part",
    )(place, received, slot.reshape(fields, 1), sym, second, filter_two, *cots)


def second_kernel(turned_ref, upper_ref, hidden_ref, out_ref, inner_ref, hid_ref):
    fields, positions = out_ref.shape
    maps, lanes = upper_ref.shape
    inner_ref[...] = dot(turned_ref[...], upper_ref[...])
    hid_ref[...] = hidden_ref[...].astype(F32)
    size = 4
    for first in range(0, positions, size * lanes):
        totals = [jnp.zeros((fields, lanes), F32)] * size
        for h in range(maps):
            inner = inner_ref[h * fields : (h + 1) * fields, :]
            for k in range(size):
                at = first + k * lanes
                totals[k] = totals[k] + hid_ref[h : h + 1, at : at + lanes] * inner
        for k in range(size):
            out_ref[:, first + k * lanes : first + (k + 1) * lanes] = totals[k]


def second_part(turned, upper, hidden):
    maps, positions = hidden.shape
    fields = turned.shape[0] // maps
    return pl.pallas_call(
        second_kernel,
        in_specs=[whole()] * 3,
        out_specs=whole(),
        out_shape=jax.ShapeDtypeStruct((fields, positions), F32),
        scratch_shapes=[
            pltpu.VMEM((maps * fields, upper.shape[1]), F32),
            pltpu.VMEM((maps, positions), F32),
        ],
        compiler_params=params(),
        cost_estimate=cost(2 * maps * fields * positions, 8 * fields * positions),
        name="second_part",
    )(turned, upper, hidden)


def embed_kernel(
    orders, slots,
    place_ref, slot_ref, sym_ref, embed_ref, lower_ref, second_ref,
    table_ref, low_ref, buf_ref,
):
    fields, positions = embed_ref.shape
    maps = lower_ref.shape[0]
    tabs, _, lanes = table_ref.shape
    width = positions // lanes
    pair = 2 * lanes
    spread = (
        lax.broadcasted_iota(jnp.int32, (tabs * slots, fields), 0) == slot_ref[...]
    ).astype(BF16)
    order = [position(orders, place_ref, t) if tabs > 1 else 0 for t in range(tabs)]
    low_ref[...] = lower_ref[...].astype(F32)
    rows = MATMUL_ROWS
    jobs = [(p, start) for p in range(width // 2) for start in range(0, maps * fields, rows)]

    def issue(number):
        p, start = jobs[number]
        x = embed_ref[:, p * pair : (p + 1) * pair]
        buf_ref[number % 2] = dot(sym_ref[start : start + rows, :], x)

    state = {}

    def consume(number):
        p, start = jobs[number]
        here = pl.ds(p * pair, pair)
        y_ref = buf_ref.at[number % 2]
        gradient = second_ref[:, here] if start == 0 else state["gradient"]
        for k in range(rows // fields):
            o = start // fields + k
            gradient = gradient + low_ref[o : o + 1, here] * y_ref[k * fields : (k + 1) * fields, :]
        state["gradient"] = gradient
        if start + rows < maps * fields:
            return
        gradient = gradient.astype(BF16)
        for k in range(2):
            table = dot(spread, gradient[:, k * lanes : (k + 1) * lanes]).astype(BF16)
            at = (2 * p + k) * slots
            for t in range(tabs):
                table_ref[order[t], at : at + slots, :] = table[t * slots : (t + 1) * slots, :]

    issue(0)
    for number in range(len(jobs)):
        if number + 1 < len(jobs):
            issue(number + 1)
        consume(number)


def embed_part(orders, slots, place, slot, sym, embed, lower, second, shape):
    fields, positions = embed.shape
    maps = lower.shape[0]
    pair = 2 * shape[2]
    return pl.pallas_call(
        functools.partial(embed_kernel, orders, slots),
        in_specs=[pl.BlockSpec(memory_space=pltpu.SMEM)] + [whole()] * 5,
        out_specs=whole(),
        out_shape=jax.ShapeDtypeStruct(shape, BF16),
        scratch_shapes=[
            pltpu.VMEM((maps, positions), F32),
            pltpu.VMEM((2, MATMUL_ROWS, pair), F32),
        ],
        compiler_params=params(),
        cost_estimate=cost(200 * maps * fields * fields * positions, 8 * embed.size),
        name="embed_part",
    )(place, slot.reshape(1, fields), sym, embed, lower, second)


def owner_kernel(orders, place_ref, table_ref, out_ref, *grads):
    width, slots, _ = out_ref.shape
    tabs, _, lanes = table_ref.shape
    for t in range(tabs):
        block = position(orders, place_ref, t)
        for d in range(width):
            out_ref[d, :, t * lanes : (t + 1) * lanes] = table_ref[
                block, d * slots : (d + 1) * slots, :
            ]
    if not grads:
        return
    one_ref, two_ref = grads
    maps = one_ref.shape[0]
    total = table_ref[0, width * slots :, :].astype(F32)
    for t in range(1, tabs):
        total = total + table_ref[t, width * slots :, :].astype(F32)
    one_ref[...] = total[:maps]
    two_ref[: maps // 2, :] = total[maps:, : lanes // 2]
    two_ref[maps // 2 :, :] = total[maps:, lanes // 2 :]


def owner_part(orders, place, table, slots, width, maps):
    tabs, rows, lanes = table.shape
    shapes = [jax.ShapeDtypeStruct((width, slots, tabs * lanes), BF16)]
    if rows > width * slots:
        shapes += [
            jax.ShapeDtypeStruct((maps, lanes), F32),
            jax.ShapeDtypeStruct((maps, lanes // 2), F32),
        ]
    results = pl.pallas_call(
        functools.partial(owner_kernel, orders),
        in_specs=[pl.BlockSpec(memory_space=pltpu.SMEM), whole()],
        out_specs=[whole()] * len(shapes),
        out_shape=shapes,
        compiler_params=params(),
        name="owner_part",
    )(place, table)
    return results[0].transpose(1, 0, 2), *results[1:]


def per_device(bag_items, lengths, field_slot, filter_one, filter_two, cotangent):
    slots, _, width, samples = bag_items.shape
    tabs = lax.axis_size("tab")
    cols = lax.axis_size("col")
    devices = tabs * cols
    lanes = samples // tabs
    maps = filter_one.shape[0]
    fields = field_slot.shape[0]
    scales = ((width * cols) ** -0.5, samples**-0.5)
    place = lax.axis_index("col").astype(jnp.int32).reshape(1)
    small = slots % 16 != 0
    packable = (
        fields * fields == devices * lanes
        and fields * 2 == lanes
        and maps == devices
        and cols & (cols - 1) == 0
        and cols > 1
        and tabs % 2 == 0
        and not small
    )
    orders = tab_orders(tabs) if packable else (list(range(tabs)),) * 2
    sent = pool(orders, place, bag_items, lengths)
    sent, cotangent = lax.optimization_barrier((sent, cotangent))
    received = exchange(sent, orders, cols)
    if cols & (cols - 1):
        cots = [lax.all_gather(cotangent, "col", axis=1, tiled=True)]
    else:
        cots = [cotangent] + [
            lax.ppermute(cotangent, "col", [(c, c ^ r) for c in range(cols)])
            for r in range(1, cols)
        ]
    square = filter_one.reshape(maps, fields, fields).astype(F32)
    sym = (square + square.transpose(0, 2, 1)).astype(BF16).reshape(maps * fields, fields)
    second = filter_two.reshape(maps * maps, fields)
    if small:
        received = received.reshape(tabs, width, slots, lanes).transpose(1, 0, 2, 3)
        received = received.reshape(1, width * tabs * slots, lanes)
    keep, away, embed, hidden, lower, upper = forward_part(
        (cols, tabs) if packable else None,
        orders, scales, place, received, field_slot, cots, sym, second, filter_two, width,
    )
    chunks, rows, _ = received.shape
    block = maps + maps // 2 if packable else 0
    table = embed_part(
        orders, rows // width, place, field_slot, sym, embed, lower,
        second_part(filter_two.T, upper, hidden), (chunks, rows, lanes),
    )
    if packable:
        total = keep.astype(F32)
        bit = 1
        while True:
            total = total + lax.ppermute(
                away, "col", [(c, c ^ bit) for c in range(cols)]
            ).astype(F32)
            bit *= 2
            if bit == cols:
                break
            half = total.shape[0] // 2
            total, away = total[:half], total[half:].astype(BF16)
        grads = total[: tabs * block].astype(BF16).reshape(tabs, block, lanes)
        table = jnp.concatenate([table, grads], axis=1)
        returned = exchange(table, orders, cols)
        pooled_grad, grad_one, grad_two = owner_part(orders, place, returned, slots, width, maps)
        share = lanes // cols
        packs = total[tabs * block :]
        pooled = jnp.concatenate(
            [packs[:, g * share : (g + 1) * share] for g in range(lanes // share)], axis=0
        )
        return (pooled, grad_one, grad_two, pooled_grad)
    if small:
        table = table.reshape(width, tabs, slots, lanes).transpose(1, 0, 2, 3)
        table = table.reshape(tabs, width * slots, lanes)
    returned = exchange(table, orders, cols)
    (pooled_grad,) = owner_part(orders, place, returned, slots, width, maps)
    pooled = lax.psum_scatter(away, "col", scatter_dimension=1, tiled=True)
    shaped = keep.reshape(fields + maps, maps, fields).transpose(1, 0, 2)
    grad_one = shaped[:, :fields].reshape(maps, tabs, cols, -1)
    grad_two = shaped[:, fields:].reshape(maps, tabs, cols, -1)
    grad_one = lax.psum_scatter(grad_one, "col", scatter_dimension=2, tiled=True)
    grad_two = lax.psum_scatter(grad_two, "col", scatter_dimension=2, tiled=True)
    grad_one = lax.psum_scatter(grad_one, "tab", scatter_dimension=1, tiled=True)
    grad_two = lax.psum_scatter(grad_two, "tab", scatter_dimension=1, tiled=True)
    return (pooled, grad_one.reshape(maps, -1), grad_two.reshape(maps, -1), pooled_grad)


def solution(mesh):
    in_specs = (P("tab", None, "col", None), P("tab", None), P(), P(), P(), P(None, ("tab", "col")))
    out_specs = (
        P(None, ("tab", "col")),
        P(None, ("tab", "col")),
        P(None, ("tab", "col")),
        P("tab", "col", None),
    )
    return jax.shard_map(
        per_device, mesh=mesh, in_specs=in_specs, out_specs=out_specs, check_vma=False
    )
```

```python
import functools

import jax
import jax.numpy as jnp
from jax import lax
from jax.experimental import pallas as pl
from jax.experimental.pallas import tpu as pltpu
from jax.sharding import PartitionSpec as P

BF16 = jnp.bfloat16
F32 = jnp.float32
VMEM_BYTES = 48 * 1024 * 1024
MATMUL_ROWS = 1024
FILTER_ROWS = 512
INNER_GROUPS = 2


def params():
    return pltpu.CompilerParams(vmem_limit_bytes=VMEM_BYTES)


def cost(flops, moved):
    return pl.CostEstimate(flops=flops, bytes_accessed=moved, transcendentals=0)


def whole():
    return pl.BlockSpec(memory_space=pltpu.VMEM)


def dot(left, right):
    return jnp.dot(left, right, preferred_element_type=F32)


def dot_lanes(left, right):
    return lax.dot_general(left, right, (((1,), (1,)), ((), ())), preferred_element_type=F32)


def tab_orders(tabs):
    first = [tabs - 1 - i // 2 if i % 2 == 0 else i // 2 for i in range(tabs)]
    return first, first[tabs // 2 :] + first[: tabs // 2]


def position(orders, place_ref, t):
    near, far = orders[0].index(t), orders[1].index(t)
    if near == far:
        return near
    return jnp.where(lax.rem(place_ref[0], 2) == 0, near, far)


def exchange(value, orders, cols):
    if orders[0] == orders[1]:
        return lax.all_to_all(value, "tab", split_axis=0, concat_axis=0, tiled=True)
    groups = [[t * cols + c for t in orders[c % 2]] for c in range(cols)]
    return lax.all_to_all(
        value, ("tab", "col"), split_axis=0, concat_axis=0, tiled=True, axis_index_groups=groups
    )


def pool_kernel(steps, orders, place_ref, bag_hbm, lengths_hbm, out_ref, bag_ref, lengths_ref, rows_ref, sems):
    slots, width, items, _ = bag_hbm.shape
    chunks, _, lanes = out_ref.shape
    per_step = chunks // steps
    counts = pltpu.make_async_copy(lengths_hbm, lengths_ref, sems.at[steps])
    counts.start()
    copies = []
    for k in range(steps):
        part = pl.ds(k * per_step * lanes, per_step * lanes)
        copy = pltpu.make_async_copy(
            bag_hbm.at[:, :, :, part], bag_ref.at[:, :, :, part], sems.at[k]
        )
        copy.start()
        copies.append(copy)
    counts.wait()
    for chunk in range(chunks):
        if chunk % per_step == 0:
            copies[chunk // per_step].wait()
        here = pl.ds(chunk * lanes, lanes)
        buffer = chunk % 2
        block = position(orders, place_ref, chunk)
        for slot in range(slots):
            at = slot * width * items
            rows_ref[buffer, at : at + width * items, :] = (
                bag_ref[slot, :, :, here].astype(F32).reshape(width * items, lanes)
            )
        count = lengths_ref[:, here]
        for d in range(width):
            total = jnp.zeros((slots, lanes), F32)
            for item in range(items):
                value = rows_ref[buffer, pl.ds(d * items + item, slots, stride=width * items), :]
                total = total + jnp.where(count > item, value, 0.0)
            out_ref[block, d * slots : (d + 1) * slots, :] = total.astype(BF16)


def pool(orders, place, bag_items, lengths):
    tab_count = len(orders[0])
    bag = bag_items.transpose(0, 2, 1, 3)
    slots, width, items, samples = bag.shape
    lanes = samples // tab_count
    steps = min(4, tab_count)
    return pl.pallas_call(
        functools.partial(pool_kernel, steps, orders),
        in_specs=[pl.BlockSpec(memory_space=pltpu.SMEM)] + [pl.BlockSpec(memory_space=pltpu.HBM)] * 2,
        out_specs=whole(),
        out_shape=jax.ShapeDtypeStruct((tab_count, width * slots, lanes), BF16),
        scratch_shapes=[
            pltpu.VMEM(bag.shape, BF16),
            pltpu.VMEM(lengths.shape, jnp.int32),
            pltpu.VMEM((2, width * (slots + 1) * items, lanes), F32),
            pltpu.SemaphoreType.DMA((steps + 1,)),
        ],
        compiler_params=pltpu.CompilerParams(vmem_limit_bytes=62 * 1024 * 1024),
        name="pool_bags",
    )(place, bag, lengths)


def forward_kernel(
    packed, orders, scales, count,
    place_ref, received_ref, slot_ref, sym_ref, second_ref, filter_ref,
    *refs,
):
    cot_refs, refs = refs[:count], refs[count:]
    outs = refs[:2]
    (
        embed_ref, hidden_ref, lower_ref, upper_ref,
        cot_ref, up_ref, x_ref, hid_ref, maps_ref, sum_ref, inner_ref, grad_ref, buf_ref, pair_ref,
        pack_ref,
    ) = refs[2:]
    fields = slot_ref.shape[0]
    maps, positions = hidden_ref.shape
    lanes = upper_ref.shape[1]
    width = positions // lanes
    tabs = received_ref.shape[0]
    slots = received_ref.shape[1] // width
    pair = 2 * lanes
    scale = scales[0]
    for r in range(count):
        cot_ref[r] = cot_refs[r][...].astype(F32)
    share = lanes // count
    for c in range(count):
        block = cot_ref[jnp.bitwise_xor(place_ref[0], c)] if count > 1 else cot_ref[0]
        up_ref[:, c * share : (c + 1) * share] = (block * scale).astype(BF16).astype(F32)
    up_ref[:, lanes:] = up_ref[:, :lanes]
    upper = up_ref[maps:, :lanes].astype(BF16)
    upper_ref[...] = upper
    onehot = (
        lax.broadcasted_iota(jnp.int32, (fields, tabs * slots), 1) == slot_ref[...]
    ).astype(BF16)
    order = [position(orders, place_ref, t) if tabs > 1 else 0 for t in range(tabs)]
    for d in range(width):
        parts = [received_ref[order[t], d * slots : (d + 1) * slots, :] for t in range(tabs)]
        x = dot(onehot, parts[0] if len(parts) == 1 else jnp.concatenate(parts, axis=0))
        x_ref[:, d * lanes : (d + 1) * lanes] = x
        embed_ref[:, d * lanes : (d + 1) * lanes] = x.astype(BF16)
    sum_ref[...] = jnp.zeros_like(sum_ref)
    rows = MATMUL_ROWS
    jobs = []
    for p in range(width // 2):
        jobs += [("z", p, start) for start in range(0, maps * maps, rows)]
        jobs += [("y", p, start) for start in range(0, maps * fields, rows)]

    def issue(number):
        kind, p, start = jobs[number]
        source = second_ref if kind == "z" else sym_ref
        x = embed_ref[:, p * pair : (p + 1) * pair]
        buf_ref[number % 2] = dot(source[start : start + rows, :], x)

    state = {}

    def consume(number):
        kind, p, start = jobs[number]
        here = pl.ds(p * pair, pair)
        b = p % 2
        y_ref = buf_ref.at[number % 2]
        if kind == "z":
            lower = up_ref[:maps, :] if start == 0 else state["lower"]
            for k in range(rows // maps):
                o = start // maps + k
                lower = lower + up_ref[maps + o : maps + o + 1, :] * y_ref[k * maps : (k + 1) * maps, :]
            state["lower"] = lower
            if start + rows == maps * maps:
                lower_ref[:, here] = lower.astype(BF16)
            return
        x_float = x_ref[:, here]
        for k in range(rows // fields):
            o = start // fields + k
            mine = y_ref[k * fields : (k + 1) * fields, :]
            maps_ref[b, o : o + 1, :] = 0.5 * jnp.sum(mine * x_float, axis=0, keepdims=True)
        if start + rows < maps * fields:
            return
        first_maps = maps_ref[b]
        sum_ref[...] += first_maps
        hidden = first_maps.astype(BF16)
        hidden_ref[:, here] = hidden
        hid_ref[:, here] = hidden.astype(F32)

    issue(0)
    for number in range(len(jobs)):
        if number + 1 < len(jobs):
            issue(number + 1)
        consume(number)

    some = FILTER_ROWS // maps
    own_col = place_ref[0]

    def products(first):
        lower = lower_ref[...].astype(F32)
        for k in range(some):
            f = first + k
            pair_ref[first // some % 2, k * maps : (k + 1) * maps, :] = (
                x_ref[f : f + 1, :] * lower
            ).astype(BF16)

    def keep_rows(k, rows, at):
        cols, tabs = packed
        c = k % cols
        at += orders[c % 2].index(k // cols) * (maps + maps // 2)
        half = rows.shape[0] // 2
        both = jnp.concatenate([rows[:half], rows[half:]], axis=1) * scales[1]
        pack_ref[jnp.bitwise_xor(own_col, c), at : at + half, :] = both.astype(BF16)

    def sums(first):
        part = dot_lanes(pair_ref[first // some % 2], embed_ref[...])
        if not packed:
            grad_ref[first * maps : (first + some) * maps, :] = part
            return
        for k in range(some // 2):
            keep_rows(first // 2 + k, part[2 * k * maps : 2 * (k + 1) * maps], 0)

    def inner(first, size):
        totals = [jnp.zeros((fields, lanes), F32)] * size
        for d in range(width):
            here = pl.ds(d * lanes, lanes)
            x = x_ref[:, here]
            for k in range(size):
                totals[k] = totals[k] + hid_ref[first + k : first + k + 1, here] * x
        for k in range(size):
            at = (first + k) * fields
            inner_ref[at : at + fields, :] = totals[k].astype(BF16)

    group, done = 4, 0
    products(0)
    for first in range(0, fields, some):
        if first + some < fields:
            products(first + some)
        for _ in range(INNER_GROUPS):
            if done < maps:
                inner(done, group)
                done += group
        sums(first)
    for done in range(done, maps, group):
        inner(done, group)
    second = dot_lanes(upper, inner_ref[...])
    two = dot(filter_ref[...], inner_ref[...])
    pooled = jnp.concatenate([sum_ref[:, :lanes] + sum_ref[:, lanes:], two], axis=0) * scale
    if not packed:
        base = fields * maps
        for h in range(maps):
            grad_ref[base + h * maps : base + (h + 1) * maps, :] = second[
                :, h * fields : (h + 1) * fields
            ]
        outs[0][...] = grad_ref[...] * scales[1]
        outs[1][...] = pooled
        return
    cols, tabs = packed
    for h in range(maps):
        keep_rows(h, second[:, h * fields : (h + 1) * fields], maps)
    tall = 2 * maps * share // lanes
    last = tabs * (maps + maps // 2)
    for c in range(cols):
        pack_ref[jnp.bitwise_xor(own_col, c), last : last + tall, :] = jnp.concatenate(
            [
                pooled[g * tall : (g + 1) * tall, c * share : (c + 1) * share]
                for g in range(lanes // share)
            ],
            axis=1,
        ).astype(BF16)
    for r in range(cols):
        outs[r % 2][r // 2 * (last + tall) : (r // 2 + 1) * (last + tall), :] = pack_ref[r]


def forward_part(packed, orders, scales, place, received, slot, cots, sym, second, filter_two, width):
    fields = slot.shape[0]
    maps = cots[0].shape[0] // 2
    lanes = cots[0].shape[1] * len(cots)
    positions = width * lanes
    pair = 2 * lanes
    grads = (fields + maps) * maps
    if packed:
        cols, tabs = packed
        tall = 2 * maps // cols
        piece = (cols // 2 * (tabs * (maps + maps // 2) + tall), lanes)
        outs = [jax.ShapeDtypeStruct(piece, BF16)] * 2
        pack = pltpu.VMEM((cols, tabs * (maps + maps // 2) + tall, lanes), BF16)
    else:
        outs = [
            jax.ShapeDtypeStruct((grads, fields), F32),
            jax.ShapeDtypeStruct((2 * maps, lanes), F32),
        ]
        pack = pltpu.VMEM((1, 16, lanes), BF16)
    return pl.pallas_call(
        functools.partial(forward_kernel, packed, orders, scales, len(cots)),
        in_specs=[pl.BlockSpec(memory_space=pltpu.SMEM)] + [whole()] * (5 + len(cots)),
        out_specs=[whole()] * 6,
        out_shape=outs
        + [
            jax.ShapeDtypeStruct((fields, positions), BF16),
            jax.ShapeDtypeStruct((maps, positions), BF16),
            jax.ShapeDtypeStruct((maps, positions), BF16),
            jax.ShapeDtypeStruct((maps, lanes), BF16),
        ],
        scratch_shapes=[
            pltpu.VMEM((len(cots),) + cots[0].shape, F32),
            pltpu.VMEM((2 * maps, pair), F32),
            pltpu.VMEM((fields, positions), F32),
            pltpu.VMEM((maps, positions), F32),
            pltpu.VMEM((2, maps, pair), F32),
            pltpu.VMEM((maps, pair), F32),
            pltpu.VMEM((maps * fields, lanes), BF16),
            pltpu.VMEM((8 if packed else grads, fields), F32),
            pltpu.VMEM((2, MATMUL_ROWS, pair), F32),
            pltpu.VMEM((2, FILTER_ROWS, positions), BF16),
            pack,
        ],
        compiler_params=params(),
        cost_estimate=cost(8 * maps * fields * fields * positions, 4 * received.size),
        name="forward_part",
    )(place, received, slot.reshape(fields, 1), sym, second, filter_two, *cots)


def second_kernel(turned_ref, upper_ref, hidden_ref, out_ref, inner_ref, hid_ref):
    fields, positions = out_ref.shape
    maps, lanes = upper_ref.shape
    inner_ref[...] = dot(turned_ref[...], upper_ref[...])
    hid_ref[...] = hidden_ref[...].astype(F32)
    size = 4
    for first in range(0, positions, size * lanes):
        totals = [jnp.zeros((fields, lanes), F32)] * size
        for h in range(maps):
            inner = inner_ref[h * fields : (h + 1) * fields, :]
            for k in range(size):
                at = first + k * lanes
                totals[k] = totals[k] + hid_ref[h : h + 1, at : at + lanes] * inner
        for k in range(size):
            out_ref[:, first + k * lanes : first + (k + 1) * lanes] = totals[k]


def second_part(turned, upper, hidden):
    maps, positions = hidden.shape
    fields = turned.shape[0] // maps
    return pl.pallas_call(
        second_kernel,
        in_specs=[whole()] * 3,
        out_specs=whole(),
        out_shape=jax.ShapeDtypeStruct((fields, positions), F32),
        scratch_shapes=[
            pltpu.VMEM((maps * fields, upper.shape[1]), F32),
            pltpu.VMEM((maps, positions), F32),
        ],
        compiler_params=params(),
        cost_estimate=cost(2 * maps * fields * positions, 8 * fields * positions),
        name="second_part",
    )(turned, upper, hidden)


def embed_kernel(
    orders, slots,
    place_ref, slot_ref, sym_ref, embed_ref, lower_ref, second_ref,
    table_ref, low_ref, buf_ref,
):
    fields, positions = embed_ref.shape
    maps = lower_ref.shape[0]
    tabs, _, lanes = table_ref.shape
    width = positions // lanes
    pair = 2 * lanes
    spread = (
        lax.broadcasted_iota(jnp.int32, (tabs * slots, fields), 0) == slot_ref[...]
    ).astype(BF16)
    order = [position(orders, place_ref, t) if tabs > 1 else 0 for t in range(tabs)]
    low_ref[...] = lower_ref[...].astype(F32)
    rows = MATMUL_ROWS
    jobs = [(p, start) for p in range(width // 2) for start in range(0, maps * fields, rows)]

    def issue(number):
        p, start = jobs[number]
        x = embed_ref[:, p * pair : (p + 1) * pair]
        buf_ref[number % 2] = dot(sym_ref[start : start + rows, :], x)

    state = {}

    def consume(number):
        p, start = jobs[number]
        here = pl.ds(p * pair, pair)
        y_ref = buf_ref.at[number % 2]
        gradient = second_ref[:, here] if start == 0 else state["gradient"]
        for k in range(rows // fields):
            o = start // fields + k
            gradient = gradient + low_ref[o : o + 1, here] * y_ref[k * fields : (k + 1) * fields, :]
        state["gradient"] = gradient
        if start + rows < maps * fields:
            return
        gradient = gradient.astype(BF16)
        for k in range(2):
            table = dot(spread, gradient[:, k * lanes : (k + 1) * lanes]).astype(BF16)
            at = (2 * p + k) * slots
            for t in range(tabs):
                table_ref[order[t], at : at + slots, :] = table[t * slots : (t + 1) * slots, :]

    issue(0)
    for number in range(len(jobs)):
        if number + 1 < len(jobs):
            issue(number + 1)
        consume(number)


def embed_part(orders, slots, place, slot, sym, embed, lower, second, shape):
    fields, positions = embed.shape
    maps = lower.shape[0]
    pair = 2 * shape[2]
    return pl.pallas_call(
        functools.partial(embed_kernel, orders, slots),
        in_specs=[pl.BlockSpec(memory_space=pltpu.SMEM)] + [whole()] * 5,
        out_specs=whole(),
        out_shape=jax.ShapeDtypeStruct(shape, BF16),
        scratch_shapes=[
            pltpu.VMEM((maps, positions), F32),
            pltpu.VMEM((2, MATMUL_ROWS, pair), F32),
        ],
        compiler_params=params(),
        cost_estimate=cost(200 * maps * fields * fields * positions, 8 * embed.size),
        name="embed_part",
    )(place, slot.reshape(1, fields), sym, embed, lower, second)


def owner_kernel(orders, place_ref, table_ref, out_ref, *grads):
    width, slots, _ = out_ref.shape
    tabs, _, lanes = table_ref.shape
    for t in range(tabs):
        block = position(orders, place_ref, t)
        for d in range(width):
            out_ref[d, :, t * lanes : (t + 1) * lanes] = table_ref[
                block, d * slots : (d + 1) * slots, :
            ]
    if not grads:
        return
    one_ref, two_ref = grads
    maps = one_ref.shape[0]
    total = table_ref[0, width * slots :, :].astype(F32)
    for t in range(1, tabs):
        total = total + table_ref[t, width * slots :, :].astype(F32)
    one_ref[...] = total[:maps]
    two_ref[: maps // 2, :] = total[maps:, : lanes // 2]
    two_ref[maps // 2 :, :] = total[maps:, lanes // 2 :]


def owner_part(orders, place, table, slots, width, maps):
    tabs, rows, lanes = table.shape
    shapes = [jax.ShapeDtypeStruct((width, slots, tabs * lanes), BF16)]
    if rows > width * slots:
        shapes += [
            jax.ShapeDtypeStruct((maps, lanes), F32),
            jax.ShapeDtypeStruct((maps, lanes // 2), F32),
        ]
    results = pl.pallas_call(
        functools.partial(owner_kernel, orders),
        in_specs=[pl.BlockSpec(memory_space=pltpu.SMEM), whole()],
        out_specs=[whole()] * len(shapes),
        out_shape=shapes,
        compiler_params=params(),
        name="owner_part",
    )(place, table)
    return results[0].transpose(1, 0, 2), *results[1:]


def per_device(bag_items, lengths, field_slot, filter_one, filter_two, cotangent):
    slots, _, width, samples = bag_items.shape
    tabs = lax.axis_size("tab")
    cols = lax.axis_size("col")
    devices = tabs * cols
    lanes = samples // tabs
    maps = filter_one.shape[0]
    fields = field_slot.shape[0]
    scales = ((width * cols) ** -0.5, samples**-0.5)
    place = lax.axis_index("col").astype(jnp.int32).reshape(1)
    small = slots % 16 != 0
    packable = (
        fields * fields == devices * lanes
        and fields * 2 == lanes
        and maps == devices
        and cols & (cols - 1) == 0
        and cols > 1
        and tabs % 2 == 0
        and not small
    )
    orders = tab_orders(tabs) if packable else (list(range(tabs)),) * 2
    sent = pool(orders, place, bag_items, lengths)
    sent, cotangent = lax.optimization_barrier((sent, cotangent))
    received = exchange(sent, orders, cols)
    if cols & (cols - 1):
        cots = [lax.all_gather(cotangent, "col", axis=1, tiled=True)]
    else:
        cots = [cotangent] + [
            lax.ppermute(cotangent, "col", [(c, c ^ r) for c in range(cols)])
            for r in range(1, cols)
        ]
    square = filter_one.reshape(maps, fields, fields).astype(F32)
    sym = (square + square.transpose(0, 2, 1)).astype(BF16).reshape(maps * fields, fields)
    second = filter_two.reshape(maps * maps, fields)
    if small:
        received = received.reshape(tabs, width, slots, lanes).transpose(1, 0, 2, 3)
        received = received.reshape(1, width * tabs * slots, lanes)
    keep, away, embed, hidden, lower, upper = forward_part(
        (cols, tabs) if packable else None,
        orders, scales, place, received, field_slot, cots, sym, second, filter_two, width,
    )
    chunks, rows, _ = received.shape
    block = maps + maps // 2 if packable else 0
    table = embed_part(
        orders, rows // width, place, field_slot, sym, embed, lower,
        second_part(filter_two.T, upper, hidden), (chunks, rows, lanes),
    )
    if packable:
        total = keep.astype(F32)
        bit = 1
        while True:
            total = total + lax.ppermute(
                away, "col", [(c, c ^ bit) for c in range(cols)]
            ).astype(F32)
            bit *= 2
            if bit == cols:
                break
            half = total.shape[0] // 2
            total, away = total[:half], total[half:].astype(BF16)
        grads = total[: tabs * block].astype(BF16).reshape(tabs, block, lanes)
        table = jnp.concatenate([table, grads], axis=1)
        returned = exchange(table, orders, cols)
        pooled_grad, grad_one, grad_two = owner_part(orders, place, returned, slots, width, maps)
        share = lanes // cols
        packs = total[tabs * block :]
        pooled = jnp.concatenate(
            [packs[:, g * share : (g + 1) * share] for g in range(lanes // share)], axis=0
        )
        return (pooled, grad_one, grad_two, pooled_grad)
    if small:
        table = table.reshape(width, tabs, slots, lanes).transpose(1, 0, 2, 3)
        table = table.reshape(tabs, width * slots, lanes)
    returned = exchange(table, orders, cols)
    (pooled_grad,) = owner_part(orders, place, returned, slots, width, maps)
    pooled = lax.psum_scatter(away, "col", scatter_dimension=1, tiled=True)
    shaped = keep.reshape(fields + maps, maps, fields).transpose(1, 0, 2)
    grad_one = shaped[:, :fields].reshape(maps, tabs, cols, -1)
    grad_two = shaped[:, fields:].reshape(maps, tabs, cols, -1)
    grad_one = lax.psum_scatter(grad_one, "col", scatter_dimension=2, tiled=True)
    grad_two = lax.psum_scatter(grad_two, "col", scatter_dimension=2, tiled=True)
    grad_one = lax.psum_scatter(grad_one, "tab", scatter_dimension=1, tiled=True)
    grad_two = lax.psum_scatter(grad_two, "tab", scatter_dimension=1, tiled=True)
    return (pooled, grad_one.reshape(maps, -1), grad_two.reshape(maps, -1), pooled_grad)


def solution(mesh):
    in_specs = (P("tab", None, "col", None), P("tab", None), P(), P(), P(), P(None, ("tab", "col")))
    out_specs = (
        P(None, ("tab", "col")),
        P(None, ("tab", "col")),
        P(None, ("tab", "col")),
        P("tab", "col", None),
    )
    return jax.shard_map(
        per_device, mesh=mesh, in_specs=in_specs, out_specs=out_specs, check_vma=False
    )
```

```python
import functools

import jax
import jax.numpy as jnp
from jax import lax
from jax.experimental import pallas as pl
from jax.experimental.pallas import tpu as pltpu
from jax.sharding import PartitionSpec as P

BF16 = jnp.bfloat16
F32 = jnp.float32
VMEM_BYTES = 48 * 1024 * 1024
MATMUL_ROWS = 1024
FILTER_ROWS = 512
INNER_GROUPS = 2


def params():
    return pltpu.CompilerParams(vmem_limit_bytes=VMEM_BYTES)


def cost(flops, moved):
    return pl.CostEstimate(flops=flops, bytes_accessed=moved, transcendentals=0)


def whole():
    return pl.BlockSpec(memory_space=pltpu.VMEM)


def dot(left, right):
    return jnp.dot(left, right, preferred_element_type=F32)


def dot_lanes(left, right):
    return lax.dot_general(left, right, (((1,), (1,)), ((), ())), preferred_element_type=F32)


def tab_orders(tabs):
    first = [tabs - 1 - i // 2 if i % 2 == 0 else i // 2 for i in range(tabs)]
    return first, first[tabs // 2 :] + first[: tabs // 2]


def position(orders, place_ref, t):
    near, far = orders[0].index(t), orders[1].index(t)
    if near == far:
        return near
    return jnp.where(lax.rem(place_ref[0], 2) == 0, near, far)


def exchange(value, orders, cols):
    if orders[0] == orders[1]:
        return lax.all_to_all(value, "tab", split_axis=0, concat_axis=0, tiled=True)
    groups = [[t * cols + c for t in orders[c % 2]] for c in range(cols)]
    return lax.all_to_all(
        value, ("tab", "col"), split_axis=0, concat_axis=0, tiled=True, axis_index_groups=groups
    )


def pool_kernel(steps, orders, place_ref, bag_hbm, lengths_hbm, out_ref, bag_ref, lengths_ref, rows_ref, sems):
    slots, width, items, _ = bag_hbm.shape
    chunks, _, lanes = out_ref.shape
    per_step = chunks // steps
    counts = pltpu.make_async_copy(lengths_hbm, lengths_ref, sems.at[steps])
    counts.start()
    copies = []
    for k in range(steps):
        part = pl.ds(k * per_step * lanes, per_step * lanes)
        copy = pltpu.make_async_copy(
            bag_hbm.at[:, :, :, part], bag_ref.at[:, :, :, part], sems.at[k]
        )
        copy.start()
        copies.append(copy)
    counts.wait()
    for chunk in range(chunks):
        if chunk % per_step == 0:
            copies[chunk // per_step].wait()
        here = pl.ds(chunk * lanes, lanes)
        buffer = chunk % 2
        block = position(orders, place_ref, chunk)
        for slot in range(slots):
            at = slot * width * items
            rows_ref[buffer, at : at + width * items, :] = (
                bag_ref[slot, :, :, here].astype(F32).reshape(width * items, lanes)
            )
        count = lengths_ref[:, here]
        for d in range(width):
            total = jnp.zeros((slots, lanes), F32)
            for item in range(items):
                value = rows_ref[buffer, pl.ds(d * items + item, slots, stride=width * items), :]
                total = total + jnp.where(count > item, value, 0.0)
            out_ref[block, d * slots : (d + 1) * slots, :] = total.astype(BF16)


def pool(orders, place, bag_items, lengths):
    tab_count = len(orders[0])
    bag = bag_items.transpose(0, 2, 1, 3)
    slots, width, items, samples = bag.shape
    lanes = samples // tab_count
    steps = min(4, tab_count)
    return pl.pallas_call(
        functools.partial(pool_kernel, steps, orders),
        in_specs=[pl.BlockSpec(memory_space=pltpu.SMEM)] + [pl.BlockSpec(memory_space=pltpu.HBM)] * 2,
        out_specs=whole(),
        out_shape=jax.ShapeDtypeStruct((tab_count, width * slots, lanes), BF16),
        scratch_shapes=[
            pltpu.VMEM(bag.shape, BF16),
            pltpu.VMEM(lengths.shape, jnp.int32),
            pltpu.VMEM((2, width * (slots + 1) * items, lanes), F32),
            pltpu.SemaphoreType.DMA((steps + 1,)),
        ],
        compiler_params=pltpu.CompilerParams(vmem_limit_bytes=62 * 1024 * 1024),
        name="pool_bags",
    )(place, bag, lengths)


def forward_kernel(
    packed, orders, scales, count,
    place_ref, received_ref, slot_ref, sym_ref, second_ref, filter_ref,
    *refs,
):
    cot_refs, refs = refs[:count], refs[count:]
    outs = refs[:2]
    (
        embed_ref, hidden_ref, lower_ref, upper_ref,
        cot_ref, up_ref, x_ref, hid_ref, maps_ref, sum_ref, inner_ref, grad_ref, buf_ref, pair_ref,
        pack_ref,
    ) = refs[2:]
    fields = slot_ref.shape[0]
    maps, positions = hidden_ref.shape
    lanes = upper_ref.shape[1]
    width = positions // lanes
    tabs = received_ref.shape[0]
    slots = received_ref.shape[1] // width
    pair = 2 * lanes
    scale = scales[0]
    for r in range(count):
        cot_ref[r] = cot_refs[r][...].astype(F32)
    share = lanes // count
    for c in range(count):
        block = cot_ref[jnp.bitwise_xor(place_ref[0], c)] if count > 1 else cot_ref[0]
        up_ref[:, c * share : (c + 1) * share] = (block * scale).astype(BF16).astype(F32)
    up_ref[:, lanes:] = up_ref[:, :lanes]
    upper = up_ref[maps:, :lanes].astype(BF16)
    upper_ref[...] = upper
    onehot = (
        lax.broadcasted_iota(jnp.int32, (fields, tabs * slots), 1) == slot_ref[...]
    ).astype(BF16)
    order = [position(orders, place_ref, t) if tabs > 1 else 0 for t in range(tabs)]
    for p in range(width // 2):
        columns = []
        for d in (2 * p, 2 * p + 1):
            parts = [received_ref[order[t], d * slots : (d + 1) * slots, :] for t in range(tabs)]
            columns.append(parts[0] if tabs == 1 else jnp.concatenate(parts, axis=0))
        x = dot(onehot, jnp.concatenate(columns, axis=1))
        x_ref[:, p * pair : (p + 1) * pair] = x
        embed_ref[:, p * pair : (p + 1) * pair] = x.astype(BF16)
    sum_ref[...] = jnp.zeros_like(sum_ref)
    rows = MATMUL_ROWS
    jobs = []
    for p in range(width // 2):
        jobs += [("z", p, start) for start in range(0, maps * maps, rows)]
        jobs += [("y", p, start) for start in range(0, maps * fields, rows)]

    def issue(number):
        kind, p, start = jobs[number]
        source = second_ref if kind == "z" else sym_ref
        x = embed_ref[:, p * pair : (p + 1) * pair]
        buf_ref[number % 2] = dot(source[start : start + rows, :], x)

    state = {}

    def consume(number):
        kind, p, start = jobs[number]
        here = pl.ds(p * pair, pair)
        b = p % 2
        y_ref = buf_ref.at[number % 2]
        if kind == "z":
            lower = up_ref[:maps, :] if start == 0 else state["lower"]
            for k in range(rows // maps):
                o = start // maps + k
                lower = lower + up_ref[maps + o : maps + o + 1, :] * y_ref[k * maps : (k + 1) * maps, :]
            state["lower"] = lower
            if start + rows == maps * maps:
                lower_ref[:, here] = lower.astype(BF16)
            return
        x_float = x_ref[:, here]
        for k in range(rows // fields):
            o = start // fields + k
            mine = y_ref[k * fields : (k + 1) * fields, :]
            maps_ref[b, o : o + 1, :] = 0.5 * jnp.sum(mine * x_float, axis=0, keepdims=True)
        if start + rows < maps * fields:
            return
        first_maps = maps_ref[b]
        sum_ref[...] += first_maps
        hidden = first_maps.astype(BF16)
        hidden_ref[:, here] = hidden
        hid_ref[:, here] = hidden.astype(F32)

    issue(0)
    for number in range(len(jobs)):
        if number + 1 < len(jobs):
            issue(number + 1)
        consume(number)

    some = FILTER_ROWS // maps
    own_col = place_ref[0]

    def products(first):
        lower = lower_ref[...].astype(F32)
        for k in range(some):
            f = first + k
            pair_ref[first // some % 2, k * maps : (k + 1) * maps, :] = (
                x_ref[f : f + 1, :] * lower
            ).astype(BF16)

    def keep_rows(k, rows, at):
        cols, tabs = packed
        c = k % cols
        at += orders[c % 2].index(k // cols) * (maps + maps // 2)
        half = rows.shape[0] // 2
        both = jnp.concatenate([rows[:half], rows[half:]], axis=1) * scales[1]
        pack_ref[jnp.bitwise_xor(own_col, c), at : at + half, :] = both.astype(BF16)

    def sums(first):
        part = dot_lanes(pair_ref[first // some % 2], embed_ref[...])
        if not packed:
            grad_ref[first * maps : (first + some) * maps, :] = part
            return
        for k in range(some // 2):
            keep_rows(first // 2 + k, part[2 * k * maps : 2 * (k + 1) * maps], 0)

    def inner(first, size):
        totals = [jnp.zeros((fields, lanes), F32)] * size
        for d in range(width):
            here = pl.ds(d * lanes, lanes)
            x = x_ref[:, here]
            for k in range(size):
                totals[k] = totals[k] + hid_ref[first + k : first + k + 1, here] * x
        for k in range(size):
            at = (first + k) * fields
            inner_ref[at : at + fields, :] = totals[k].astype(BF16)

    group, done = 4, 0
    products(0)
    for first in range(0, fields, some):
        if first + some < fields:
            products(first + some)
        for _ in range(INNER_GROUPS):
            if done < maps:
                inner(done, group)
                done += group
        sums(first)
    for done in range(done, maps, group):
        inner(done, group)
    second = dot_lanes(upper, inner_ref[...])
    two = dot(filter_ref[...], inner_ref[...])
    pooled = jnp.concatenate([sum_ref[:, :lanes] + sum_ref[:, lanes:], two], axis=0) * scale
    if not packed:
        base = fields * maps
        for h in range(maps):
            grad_ref[base + h * maps : base + (h + 1) * maps, :] = second[
                :, h * fields : (h + 1) * fields
            ]
        outs[0][...] = grad_ref[...] * scales[1]
        outs[1][...] = pooled
        return
    cols, tabs = packed
    for h in range(maps):
        keep_rows(h, second[:, h * fields : (h + 1) * fields], maps)
    tall = 2 * maps * share // lanes
    last = tabs * (maps + maps // 2)
    for c in range(cols):
        pack_ref[jnp.bitwise_xor(own_col, c), last : last + tall, :] = jnp.concatenate(
            [
                pooled[g * tall : (g + 1) * tall, c * share : (c + 1) * share]
                for g in range(lanes // share)
            ],
            axis=1,
        ).astype(BF16)
    for r in range(cols):
        outs[r % 2][r // 2 * (last + tall) : (r // 2 + 1) * (last + tall), :] = pack_ref[r]


def forward_part(packed, orders, scales, place, received, slot, cots, sym, second, filter_two, width):
    fields = slot.shape[0]
    maps = cots[0].shape[0] // 2
    lanes = cots[0].shape[1] * len(cots)
    positions = width * lanes
    pair = 2 * lanes
    grads = (fields + maps) * maps
    if packed:
        cols, tabs = packed
        tall = 2 * maps // cols
        piece = (cols // 2 * (tabs * (maps + maps // 2) + tall), lanes)
        outs = [jax.ShapeDtypeStruct(piece, BF16)] * 2
        pack = pltpu.VMEM((cols, tabs * (maps + maps // 2) + tall, lanes), BF16)
    else:
        outs = [
            jax.ShapeDtypeStruct((grads, fields), F32),
            jax.ShapeDtypeStruct((2 * maps, lanes), F32),
        ]
        pack = pltpu.VMEM((1, 16, lanes), BF16)
    return pl.pallas_call(
        functools.partial(forward_kernel, packed, orders, scales, len(cots)),
        in_specs=[pl.BlockSpec(memory_space=pltpu.SMEM)] + [whole()] * (5 + len(cots)),
        out_specs=[whole()] * 6,
        out_shape=outs
        + [
            jax.ShapeDtypeStruct((fields, positions), BF16),
            jax.ShapeDtypeStruct((maps, positions), BF16),
            jax.ShapeDtypeStruct((maps, positions), BF16),
            jax.ShapeDtypeStruct((maps, lanes), BF16),
        ],
        scratch_shapes=[
            pltpu.VMEM((len(cots),) + cots[0].shape, F32),
            pltpu.VMEM((2 * maps, pair), F32),
            pltpu.VMEM((fields, positions), F32),
            pltpu.VMEM((maps, positions), F32),
            pltpu.VMEM((2, maps, pair), F32),
            pltpu.VMEM((maps, pair), F32),
            pltpu.VMEM((maps * fields, lanes), BF16),
            pltpu.VMEM((8 if packed else grads, fields), F32),
            pltpu.VMEM((2, MATMUL_ROWS, pair), F32),
            pltpu.VMEM((2, FILTER_ROWS, positions), BF16),
            pack,
        ],
        compiler_params=params(),
        cost_estimate=cost(8 * maps * fields * fields * positions, 4 * received.size),
        name="forward_part",
    )(place, received, slot.reshape(fields, 1), sym, second, filter_two, *cots)


def second_kernel(turned_ref, upper_ref, hidden_ref, out_ref, inner_ref, hid_ref):
    fields, positions = out_ref.shape
    maps, lanes = upper_ref.shape
    inner_ref[...] = dot(turned_ref[...], upper_ref[...])
    hid_ref[...] = hidden_ref[...].astype(F32)
    size = 4
    for first in range(0, positions, size * lanes):
        totals = [jnp.zeros((fields, lanes), F32)] * size
        for h in range(maps):
            inner = inner_ref[h * fields : (h + 1) * fields, :]
            for k in range(size):
                at = first + k * lanes
                totals[k] = totals[k] + hid_ref[h : h + 1, at : at + lanes] * inner
        for k in range(size):
            out_ref[:, first + k * lanes : first + (k + 1) * lanes] = totals[k]


def second_part(turned, upper, hidden):
    maps, positions = hidden.shape
    fields = turned.shape[0] // maps
    return pl.pallas_call(
        second_kernel,
        in_specs=[whole()] * 3,
        out_specs=whole(),
        out_shape=jax.ShapeDtypeStruct((fields, positions), F32),
        scratch_shapes=[
            pltpu.VMEM((maps * fields, upper.shape[1]), F32),
            pltpu.VMEM((maps, positions), F32),
        ],
        compiler_params=params(),
        cost_estimate=cost(2 * maps * fields * positions, 8 * fields * positions),
        name="second_part",
    )(turned, upper, hidden)


def embed_kernel(
    orders, slots,
    place_ref, slot_ref, sym_ref, embed_ref, lower_ref, second_ref,
    table_ref, low_ref, buf_ref,
):
    fields, positions = embed_ref.shape
    maps = lower_ref.shape[0]
    tabs, _, lanes = table_ref.shape
    width = positions // lanes
    pair = 2 * lanes
    spread = (
        lax.broadcasted_iota(jnp.int32, (tabs * slots, fields), 0) == slot_ref[...]
    ).astype(BF16)
    order = [position(orders, place_ref, t) if tabs > 1 else 0 for t in range(tabs)]
    low_ref[...] = lower_ref[...].astype(F32)
    rows = MATMUL_ROWS
    jobs = [(p, start) for p in range(width // 2) for start in range(0, maps * fields, rows)]

    def issue(number):
        p, start = jobs[number]
        x = embed_ref[:, p * pair : (p + 1) * pair]
        buf_ref[number % 2] = dot(sym_ref[start : start + rows, :], x)

    state = {}

    def consume(number):
        p, start = jobs[number]
        here = pl.ds(p * pair, pair)
        y_ref = buf_ref.at[number % 2]
        gradient = second_ref[:, here] if start == 0 else state["gradient"]
        for k in range(rows // fields):
            o = start // fields + k
            gradient = gradient + low_ref[o : o + 1, here] * y_ref[k * fields : (k + 1) * fields, :]
        state["gradient"] = gradient
        if start + rows < maps * fields:
            return
        gradient = gradient.astype(BF16)
        table = dot(spread, gradient).astype(BF16)
        for k in range(2):
            at = (2 * p + k) * slots
            for t in range(tabs):
                table_ref[order[t], at : at + slots, :] = table[
                    t * slots : (t + 1) * slots, k * lanes : (k + 1) * lanes
                ]

    issue(0)
    for number in range(len(jobs)):
        if number + 1 < len(jobs):
            issue(number + 1)
        consume(number)


def embed_part(orders, slots, place, slot, sym, embed, lower, second, shape):
    fields, positions = embed.shape
    maps = lower.shape[0]
    pair = 2 * shape[2]
    return pl.pallas_call(
        functools.partial(embed_kernel, orders, slots),
        in_specs=[pl.BlockSpec(memory_space=pltpu.SMEM)] + [whole()] * 5,
        out_specs=whole(),
        out_shape=jax.ShapeDtypeStruct(shape, BF16),
        scratch_shapes=[
            pltpu.VMEM((maps, positions), F32),
            pltpu.VMEM((2, MATMUL_ROWS, pair), F32),
        ],
        compiler_params=params(),
        cost_estimate=cost(200 * maps * fields * fields * positions, 8 * embed.size),
        name="embed_part",
    )(place, slot.reshape(1, fields), sym, embed, lower, second)


def owner_kernel(orders, place_ref, table_ref, out_ref, *grads):
    width, slots, _ = out_ref.shape
    tabs, _, lanes = table_ref.shape
    for t in range(tabs):
        block = position(orders, place_ref, t)
        for d in range(width):
            out_ref[d, :, t * lanes : (t + 1) * lanes] = table_ref[
                block, d * slots : (d + 1) * slots, :
            ]
    if not grads:
        return
    one_ref, two_ref = grads
    maps = one_ref.shape[0]
    total = table_ref[0, width * slots :, :].astype(F32)
    for t in range(1, tabs):
        total = total + table_ref[t, width * slots :, :].astype(F32)
    one_ref[...] = total[:maps]
    two_ref[: maps // 2, :] = total[maps:, : lanes // 2]
    two_ref[maps // 2 :, :] = total[maps:, lanes // 2 :]


def owner_part(orders, place, table, slots, width, maps):
    tabs, rows, lanes = table.shape
    shapes = [jax.ShapeDtypeStruct((width, slots, tabs * lanes), BF16)]
    if rows > width * slots:
        shapes += [
            jax.ShapeDtypeStruct((maps, lanes), F32),
            jax.ShapeDtypeStruct((maps, lanes // 2), F32),
        ]
    results = pl.pallas_call(
        functools.partial(owner_kernel, orders),
        in_specs=[pl.BlockSpec(memory_space=pltpu.SMEM), whole()],
        out_specs=[whole()] * len(shapes),
        out_shape=shapes,
        compiler_params=params(),
        name="owner_part",
    )(place, table)
    return results[0].transpose(1, 0, 2), *results[1:]


def per_device(bag_items, lengths, field_slot, filter_one, filter_two, cotangent):
    slots, _, width, samples = bag_items.shape
    tabs = lax.axis_size("tab")
    cols = lax.axis_size("col")
    devices = tabs * cols
    lanes = samples // tabs
    maps = filter_one.shape[0]
    fields = field_slot.shape[0]
    scales = ((width * cols) ** -0.5, samples**-0.5)
    place = lax.axis_index("col").astype(jnp.int32).reshape(1)
    small = slots % 16 != 0
    packable = (
        fields * fields == devices * lanes
        and fields * 2 == lanes
        and maps == devices
        and cols & (cols - 1) == 0
        and cols > 1
        and tabs % 2 == 0
        and not small
    )
    orders = tab_orders(tabs) if packable else (list(range(tabs)),) * 2
    sent = pool(orders, place, bag_items, lengths)
    sent, cotangent = lax.optimization_barrier((sent, cotangent))
    received = exchange(sent, orders, cols)
    if cols & (cols - 1):
        cots = [lax.all_gather(cotangent, "col", axis=1, tiled=True)]
    else:
        cots = [cotangent] + [
            lax.ppermute(cotangent, "col", [(c, c ^ r) for c in range(cols)])
            for r in range(1, cols)
        ]
    square = filter_one.reshape(maps, fields, fields).astype(F32)
    sym = (square + square.transpose(0, 2, 1)).astype(BF16).reshape(maps * fields, fields)
    second = filter_two.reshape(maps * maps, fields)
    if small:
        received = received.reshape(tabs, width, slots, lanes).transpose(1, 0, 2, 3)
        received = received.reshape(1, width * tabs * slots, lanes)
    keep, away, embed, hidden, lower, upper = forward_part(
        (cols, tabs) if packable else None,
        orders, scales, place, received, field_slot, cots, sym, second, filter_two, width,
    )
    chunks, rows, _ = received.shape
    block = maps + maps // 2 if packable else 0
    table = embed_part(
        orders, rows // width, place, field_slot, sym, embed, lower,
        second_part(filter_two.T, upper, hidden), (chunks, rows, lanes),
    )
    if packable:
        total = keep.astype(F32)
        bit = 1
        while True:
            total = total + lax.ppermute(
                away, "col", [(c, c ^ bit) for c in range(cols)]
            ).astype(F32)
            bit *= 2
            if bit == cols:
                break
            half = total.shape[0] // 2
            total, away = total[:half], total[half:].astype(BF16)
        grads = total[: tabs * block].astype(BF16).reshape(tabs, block, lanes)
        table = jnp.concatenate([table, grads], axis=1)
        returned = exchange(table, orders, cols)
        pooled_grad, grad_one, grad_two = owner_part(orders, place, returned, slots, width, maps)
        share = lanes // cols
        packs = total[tabs * block :]
        pooled = jnp.concatenate(
            [packs[:, g * share : (g + 1) * share] for g in range(lanes // share)], axis=0
        )
        return (pooled, grad_one, grad_two, pooled_grad)
    if small:
        table = table.reshape(width, tabs, slots, lanes).transpose(1, 0, 2, 3)
        table = table.reshape(tabs, width * slots, lanes)
    returned = exchange(table, orders, cols)
    (pooled_grad,) = owner_part(orders, place, returned, slots, width, maps)
    pooled = lax.psum_scatter(away, "col", scatter_dimension=1, tiled=True)
    shaped = keep.reshape(fields + maps, maps, fields).transpose(1, 0, 2)
    grad_one = shaped[:, :fields].reshape(maps, tabs, cols, -1)
    grad_two = shaped[:, fields:].reshape(maps, tabs, cols, -1)
    grad_one = lax.psum_scatter(grad_one, "col", scatter_dimension=2, tiled=True)
    grad_two = lax.psum_scatter(grad_two, "col", scatter_dimension=2, tiled=True)
    grad_one = lax.psum_scatter(grad_one, "tab", scatter_dimension=1, tiled=True)
    grad_two = lax.psum_scatter(grad_two, "tab", scatter_dimension=1, tiled=True)
    return (pooled, grad_one.reshape(maps, -1), grad_two.reshape(maps, -1), pooled_grad)


def solution(mesh):
    in_specs = (P("tab", None, "col", None), P("tab", None), P(), P(), P(), P(None, ("tab", "col")))
    out_specs = (
        P(None, ("tab", "col")),
        P(None, ("tab", "col")),
        P(None, ("tab", "col")),
        P("tab", "col", None),
    )
    return jax.shard_map(
        per_device, mesh=mesh, in_specs=in_specs, out_specs=out_specs, check_vma=False
    )
```
